32 devices in a mesh: outer: 2 (over core), inner: 16 (over z, y, x).
Axes of the slice: x: 2, y: 2, z: 4, core: 2. Of those that a mesh axis runs over, the one named last changes fastest.
Arguments:
- features: float32 [65536, 1024], P(('outer', 'inner'))
- dest: int32 [512], P(('outer', 'inner')), may hold values from 0 to 15, as said below
- slot: int32 [512], P(('outer', 'inner')), may hold values from 0 to 15, as said below
Outputs:
- standardized: float32 [65536, 1024], P(('outer', 'inner'))
- moments: float32 [2, 1024], replicated
The draws below stay inside these ranges and needn't reach their ends.
Inputs may be any that keep to these rules, and one draw needn't show every extreme that they name: `dest`: blocks of one device name destinations in the same shuffle domain; from one device at most 1 block go to any one destination, and exactly 1 to each destination it names. Every device of a shuffle domain receives exactly 16 blocks, each with a different slot.
All inputs are finite; a program needn't handle non-finite values.
Results may differ from the reference program's by a relative error of at most 0.000031.
Values sent between devices are 32-bit elements; how exact they have to be, the bound alone decides.
No kernel may reach another device: no remote copies, remote signals or barrier semaphores. Data moves between devices by JAX's collectives and lax.ppermute only.
A program may use at most 128 MiB of HBM per device.

```python
import jax
import jax.numpy as jnp
from jax import lax

F = 1024
ROWS_DEV = 2048
BLOCK = 128
BLK_DEV = 16
PEERS = 16
ROWS = 65536
BLOCKS = 512
DEVICES = 32


def route_table(key):
    group_total = BLOCKS // (PEERS * BLK_DEV)

    def one_group(group):
        group_key = jax.random.fold_in(jax.random.fold_in(key, 7), group)
        offsets = jax.random.permutation(jax.random.fold_in(group_key, 1), PEERS)
        ordering = jax.random.permutation(jax.random.fold_in(group_key, 2), BLK_DEV)
        turning = jax.random.permutation(jax.random.fold_in(group_key, 3), BLK_DEV)
        relabel = jax.random.permutation(jax.random.fold_in(group_key, 4), PEERS)
        inverse = jnp.argsort(relabel)
        offset_of = offsets[ordering % PEERS]
        sources = jnp.arange(PEERS)
        targets = relabel[(inverse[sources][:, None] + offset_of[None, :]) % PEERS]
        slot_table = (turning[None, :] + targets) % BLK_DEV
        return (targets.reshape(-1), slot_table.reshape(-1))
    targets, slot_table = jax.vmap(one_group)(jnp.arange(group_total))
    return (targets.reshape(-1).astype(jnp.int32), slot_table.reshape(-1).astype(jnp.int32))


def draw_dest(key, part):
    return route_table(key)[0]


def draw_slot(key, part):
    return route_table(key)[1]


def draw_features(key, part):
    column_scale = 10.0 ** jax.random.uniform(jax.random.fold_in(key, 1), (1, F))
    column_shift = 3.0 * jax.random.normal(jax.random.fold_in(key, 2), (1, F))
    row_scale = 10.0 ** jax.random.uniform(jax.random.fold_in(key, 3), (ROWS, 1))
    progress = jnp.arange(ROWS, dtype=jnp.float32)[:, None] / (ROWS - 1)
    jitter = jnp.clip(jax.random.normal(jax.random.fold_in(key, 5), (ROWS, F)), -6.0, 6.0)
    values = column_shift + column_scale * (6.0 + 12.0 * progress + row_scale * jitter)
    return values.astype(jnp.float32)


def setup_inputs(seed: int = 0) -> dict:
    arg_keys = jax.random.split(jax.random.key(seed), 4)
    return {
        "features": draw_features(jax.random.fold_in(arg_keys[3], 71), 0),
        "dest": draw_dest(jax.random.fold_in(arg_keys[3], 71), 0),
        "slot": draw_slot(jax.random.fold_in(arg_keys[3], 71), 0),
    }


eps_value = 1e-06
clip_value = 3.0

def merge_pair(center_a, spread_a, center_b, spread_b, half):
    gap = center_b - center_a
    return ((center_a + center_b) * 0.5, spread_a + spread_b + gap * gap * half)

def merge_levels(centers, spreads, row_count):
    level_count = row_count
    while centers.shape[0] > 1:
        paired_c = centers.reshape(-1, 2, centers.shape[1])
        paired_s = spreads.reshape(-1, 2, spreads.shape[1])
        centers, spreads = merge_pair(paired_c[:, 0], paired_s[:, 0], paired_c[:, 1], paired_s[:, 1], level_count * 0.5)
        level_count = level_count * 2
    return (centers[0], spreads[0])

def local_moments(block_rows):
    center = lax.optimization_barrier(jnp.mean(block_rows, axis=0))
    deviation = block_rows - center
    return (center, lax.optimization_barrier(jnp.sum(deviation * deviation, axis=0)))

def standardize(block_rows, center, factor):
    return jnp.clip((block_rows - center) * factor, -clip_value, clip_value)

def reference(features, dest, slot):
    total_rows = features.shape[0]
    shards = features.reshape(DEVICES, ROWS_DEV, F)
    centers, spreads = lax.map(local_moments, shards)
    center, spread = merge_levels(centers, spreads, ROWS_DEV)
    variance = spread / total_rows
    factor = lax.rsqrt(variance + eps_value)
    scaled = lax.map(lambda block_rows: standardize(block_rows, center, factor), shards)
    group_size = PEERS * BLK_DEV
    block_ids = jnp.arange(BLOCKS, dtype=jnp.int32)
    target = block_ids // group_size * group_size + dest.astype(jnp.int32) * BLK_DEV + slot.astype(jnp.int32)
    placed = jnp.zeros((BLOCKS, BLOCK, F), jnp.float32).at[target].set(scaled.reshape(BLOCKS, BLOCK, F))
    return (placed.reshape(total_rows, F), jnp.stack([center, variance]))
```

```python
import functools

import jax
import jax.numpy as jnp
from jax import lax
from jax.experimental import pallas as pl
from jax.experimental.pallas import tpu as pltpu
from jax.sharding import PartitionSpec as P

eps_value = 1e-06
clip_value = 3.0
payload_rows = 4


def merge_pair(center_a, spread_a, center_b, spread_b, half):
    gap = center_b - center_a
    return ((center_a + center_b) * 0.5, spread_a + spread_b + gap * gap * half)


def invert(dest_ref, inverse):
    me = lax.axis_index("inner")

    def step(b, carry):
        inverse[dest_ref[b] ^ me] = b
        return carry

    lax.fori_loop(0, dest_ref.shape[0], step, 0)


def first_kernel(lanes, dest_ref, blocks_ref, *rest):
    outs, (inverse, sems) = rest[: len(lanes)], rest[len(lanes) :]
    invert(dest_ref, inverse)
    copies = [pltpu.make_async_copy(blocks_ref.at[inverse[lane]], out, sems.at[i]) for i, (lane, out) in enumerate(zip(lanes, outs))]
    for copy in copies:
        copy.start()
    for copy in copies:
        copy.wait()


def pick_first(lanes, dest, blocks):
    return pl.pallas_call(
        functools.partial(first_kernel, lanes),
        out_shape=[jax.ShapeDtypeStruct(blocks.shape[1:], blocks.dtype)] * len(lanes),
        in_specs=[pl.BlockSpec(memory_space=pltpu.SMEM), pl.BlockSpec(memory_space=pl.ANY)],
        out_specs=[pl.BlockSpec(memory_space=pl.ANY)] * len(lanes),
        scratch_shapes=[pltpu.SMEM((dest.shape[0],), jnp.int32), pltpu.SemaphoreType.DMA((len(lanes),))],
        name="pick_first",
    )(dest, blocks)


def rest_kernel(order, written, dest_ref, slot_ref, blocks_ref, payload_ref, *rest):
    outs, (held, inverse, in_sems, out_sems) = rest[: len(written)], rest[len(written) :]
    peers, rows, feats = held.shape
    row_count = peers * rows
    invert(dest_ref, inverse)
    for i, lane in enumerate(order):
        pltpu.make_async_copy(blocks_ref.at[inverse[lane]], held.at[i], in_sems.at[i]).start()

    def block_sum(i, fn):
        return jnp.sum(fn(held[i]).reshape(rows // 8, 8, feats), axis=0)

    total = jnp.zeros((8, feats), jnp.float32)
    for i, lane in enumerate(order):
        pltpu.make_async_copy(blocks_ref.at[inverse[lane]], held.at[i], in_sems.at[i]).wait()
        if lane in written:
            j = written.index(lane)
            pltpu.make_async_copy(held.at[i], outs[j], out_sems.at[j]).start()
        total = total + block_sum(i, lambda x: x)
    center = jnp.sum(total, axis=0, keepdims=True) / row_count

    def deviation(x):
        gap = x - center
        return gap * gap

    total = lax.fori_loop(0, peers, lambda i, acc: acc + block_sum(i, deviation), jnp.zeros((8, feats), jnp.float32))
    spread = jnp.sum(total, axis=0, keepdims=True)
    me = lax.axis_index("inner")
    for lane in range(peers):
        mark = jnp.full((payload_rows - 2, feats), slot_ref[inverse[lane]].astype(jnp.float32))
        payload_ref[lane ^ me] = jnp.concatenate([center, spread, mark], axis=0)
    for j in range(len(written)):
        pltpu.make_async_copy(held.at[order.index(written[j])], outs[j], out_sems.at[j]).wait()


def pick_rest(order, written, dest, slot, blocks):
    peers, rows, feats = blocks.shape
    smem, hbm = pl.BlockSpec(memory_space=pltpu.SMEM), pl.BlockSpec(memory_space=pl.ANY)
    res = pl.pallas_call(
        functools.partial(rest_kernel, order, written),
        out_shape=[jax.ShapeDtypeStruct((peers, payload_rows, feats), jnp.float32)]
        + [jax.ShapeDtypeStruct((rows, feats), blocks.dtype)] * len(written),
        in_specs=[smem, smem, hbm],
        out_specs=[pl.BlockSpec(memory_space=pltpu.VMEM)] + [hbm] * len(written),
        scratch_shapes=[
            pltpu.VMEM((peers, rows, feats), jnp.float32),
            pltpu.SMEM((peers,), jnp.int32),
            pltpu.SemaphoreType.DMA((peers,)),
            pltpu.SemaphoreType.DMA((len(written),)),
        ],
        compiler_params=pltpu.CompilerParams(vmem_limit_bytes=32 * 1024 * 1024),
        name="pick_rest",
    )(dest, slot, blocks)
    return res[0], res[1:]


def standardize(block_rows, center, factor):
    return jnp.clip((block_rows - center) * factor, -clip_value, clip_value)


def body(features, dest, slot):
    row_count, feat_width = features.shape
    peers = dest.shape[0]
    rows = row_count // peers
    outer_count = lax.axis_size("outer")
    total_rows = row_count * peers * outer_count
    blocks = features.reshape(peers, rows, feat_width)
    me = lax.axis_index("inner")

    far, near = list(range(peers // 2, peers)), list(range(1, peers // 2))
    lanes = [far[0]]
    for f, n in zip(far[1:], near):
        lanes += [n, f]
    first, later = lanes[:1], lanes[1:]
    picked = dict(zip(first, pick_first(first, dest, blocks)))
    order = later + [0] + first
    payload, rest = pick_rest(order, later + [0], dest, slot, blocks)
    picked.update(zip(later + [0], rest))

    def send(lane, block):
        return lax.ppermute(block, "inner", [(i, i ^ lane) for i in range(peers)])

    received = {lane: send(lane, picked[lane]) for lane in lanes}

    told = lax.all_to_all(payload, "inner", split_axis=0, concat_axis=0, tiled=True)
    got_slot = told[:, 2, 0].astype(jnp.int32)
    level_count = row_count
    centers, spreads = told[:, 0], told[:, 1]
    while centers.shape[0] > 1:
        centers, spreads = merge_pair(centers[0::2], spreads[0::2], centers[1::2], spreads[1::2], level_count * 0.5)
        level_count *= 2
    pair = jnp.concatenate([centers, spreads], axis=0)
    for bit in range(outer_count.bit_length() - 1):
        other = lax.ppermute(pair, "outer", [(i, i ^ 1 << bit) for i in range(outer_count)])
        center, spread = merge_pair(pair[0], pair[1], other[0], other[1], level_count * 0.5)
        level_count *= 2
        pair = jnp.stack([center, spread])
    center, variance = pair[0], pair[1] / total_rows
    factor = lax.rsqrt(variance + eps_value)

    by_lane = got_slot[me ^ jnp.arange(peers, dtype=jnp.int32)]
    out = jnp.zeros((row_count, feat_width), jnp.float32)
    for lane in [0] + lanes:
        block = picked[0] if lane == 0 else received[lane]
        out = lax.dynamic_update_slice(out, standardize(block, center, factor), (by_lane[lane] * rows, 0))
    return (out, jnp.stack([center, variance]))


def solution(mesh):
    in_specs = (P(("outer", "inner"), None), P(("outer", "inner")), P(("outer", "inner")))
    out_specs = (P(("outer", "inner"), None), P())
    return jax.shard_map(body, mesh=mesh, in_specs=in_specs, out_specs=out_specs, check_vma=False)
```

```python
import functools

import jax
import jax.numpy as jnp
from jax import lax
from jax.experimental import pallas as pl
from jax.experimental.pallas import tpu as pltpu
from jax.sharding import PartitionSpec as P

eps_value = 1e-06
clip_value = 3.0
payload_rows = 4
window = 4
in_smem, in_vmem = pl.BlockSpec(memory_space=pltpu.SMEM), pl.BlockSpec(memory_space=pltpu.VMEM)
in_hbm, in_any = pl.BlockSpec(memory_space=pltpu.HBM), pl.BlockSpec(memory_space=pl.ANY)


def merge_pair(center_a, spread_a, center_b, spread_b, half):
    gap = center_b - center_a
    return ((center_a + center_b) * 0.5, spread_a + spread_b + gap * gap * half)


def pin(array, space=pltpu.HBM):
    return pltpu.with_memory_space_constraint(array, space)


def lane_order(peers):
    half = peers // 2
    far = list(range(0, half, 2)) + list(range(1, half, 2))
    near = list(range(1, half, 2)) + list(range(2, half, 2)) + [0]
    return [lane for f, n in zip(far, near) for lane in (half + f, n)]


def lane_base(peers):
    return lax.axis_index("inner") ^ ((lax.axis_index("outer") & 1) * (peers // 2))


def first_kernel(lanes, dest_ref, features_ref, inverse_ref, *rest):
    outs, sems = rest[:-1], rest[-1]
    peers, rows = dest_ref.shape[0], outs[0].shape[0]
    base = lane_base(peers)
    for b in range(peers):
        inverse_ref[dest_ref[b] ^ base] = b
    copies = []
    for i, lane in enumerate(lanes):
        start = pl.multiple_of(inverse_ref[lane] * rows, 8)
        copies.append(pltpu.make_async_copy(features_ref.at[pl.ds(start, rows)], outs[i], sems.at[i]))
        copies[-1].start()
    for copy in copies:
        copy.wait()


def pick_first(lanes, dest, features):
    count, (row_count, feats) = len(lanes), features.shape
    rows = row_count // dest.shape[0]
    res = pl.pallas_call(
        functools.partial(first_kernel, lanes),
        out_shape=[jax.ShapeDtypeStruct(dest.shape, jnp.int32)] + [pltpu.VMEM((rows, feats), features.dtype)] * count,
        in_specs=[in_smem, in_hbm],
        out_specs=[in_smem] + [in_vmem] * count,
        scratch_shapes=[pltpu.SemaphoreType.DMA((count,))],
        name="pick_first",
    )(dest, pin(features))
    return res[0], res[1:]


def rest_kernel(lanes, first, inverse_ref, slot_ref, features_ref, payload_ref, *rest):
    outs, (held, in_sems, out_sems) = rest[: len(lanes)], rest[len(lanes) :]
    peers, rows, feats = held.shape
    base = lane_base(peers)
    order = lanes + first
    fetches = []
    for lane in order:
        start = pl.multiple_of(inverse_ref[lane] * rows, 8)
        fetches.append(pltpu.make_async_copy(features_ref.at[pl.ds(start, rows)], held.at[lane], in_sems.at[lane]))
        fetches[-1].start()

    def fold(x):
        return jnp.sum(x.reshape(rows // 8, 8, feats), axis=0)

    stores, parts = [], []
    for i, lane in enumerate(order):
        fetches[i].wait()
        if i < len(lanes):
            stores.append(pltpu.make_async_copy(held.at[lane], outs[i], out_sems.at[i]))
            stores[-1].start()
        center = jnp.sum(fold(held[lane]), axis=0, keepdims=True) / rows
        gap = held[lane] - center
        parts.append((center, jnp.sum(fold(gap * gap), axis=0, keepdims=True)))
    level_count = rows
    while len(parts) > 1:
        parts = [merge_pair(*parts[i], *parts[i + 1], level_count * 0.5) for i in range(0, len(parts), 2)]
        level_count *= 2
    for lane in range(peers):
        mark = jnp.full((payload_rows - 2, feats), slot_ref[inverse_ref[lane]].astype(jnp.float32))
        payload_ref[lane ^ base] = jnp.concatenate(list(parts[0]) + [mark], axis=0)
    for store in stores:
        store.wait()


def pick_rest(lanes, first, inverse, slot, features):
    peers, (row_count, feats) = inverse.shape[0], features.shape
    rows = row_count // peers
    res = pl.pallas_call(
        functools.partial(rest_kernel, lanes, first),
        out_shape=[jax.ShapeDtypeStruct((peers, payload_rows, feats), jnp.float32)] + [pltpu.HBM((rows, feats), features.dtype)] * len(lanes),
        in_specs=[in_smem, in_smem, in_hbm],
        out_specs=[in_vmem] + [in_hbm] * len(lanes),
        scratch_shapes=[
            pltpu.VMEM((peers, rows, feats), jnp.float32),
            pltpu.SemaphoreType.DMA((peers,)),
            pltpu.SemaphoreType.DMA((len(lanes),)),
        ],
        compiler_params=pltpu.CompilerParams(vmem_limit_bytes=32 * 1024 * 1024),
        cost_estimate=pl.CostEstimate(flops=6 * features.size, bytes_accessed=8 * features.size, transcendentals=0),
        name="pick_rest",
    )(inverse, slot, pin(features))
    return res[0], res[1:]


def place_kernel(lanes, near_by, slot_ref, scale_ref, *rest):
    blocks, (out_ref, held, in_sems, out_sems) = rest[: len(lanes)], rest[-4:]
    _, parts, part_rows, _ = held.shape
    plan = []
    for n, lane in enumerate(lanes):
        start = slot_ref[lane] * (parts * part_rows)
        for i in range(parts):
            target = pl.ds(pl.multiple_of(start + i * part_rows, 8), part_rows)
            source = blocks[n].at[pl.ds(i * part_rows, part_rows)]
            fetch = None if near_by else pltpu.make_async_copy(source, held.at[n, i], in_sems.at[n, i])
            if fetch is not None:
                fetch.start()
            plan.append((n, i, source, fetch, pltpu.make_async_copy(held.at[n, i], out_ref.at[target], out_sems.at[n, i])))
    center, factor = scale_ref[0:1], scale_ref[1:2]
    for n, i, source, fetch, store in plan:
        if fetch is not None:
            fetch.wait()
        values = source[...] if fetch is None else held[n, i]
        held[n, i] = jnp.clip((values - center) * factor, -clip_value, clip_value)
        store.start()
    for *_, store in plan:
        store.wait()


def place(lanes, blocks, slots, scale, out, row_count, near_by):
    rows, feats = blocks[0].shape
    count, parts = len(lanes), max(1, rows // 32)
    space, spec = (pltpu.VMEM, in_vmem) if near_by else (pltpu.HBM, in_hbm)
    args = [slots, scale] + [pin(block, space) for block in blocks] + ([] if out is None else [pin(out)])
    return pl.pallas_call(
        functools.partial(place_kernel, lanes, near_by),
        out_shape=pltpu.HBM((row_count, feats), jnp.float32),
        in_specs=[in_smem, in_vmem] + [spec] * count + ([] if out is None else [in_hbm]),
        out_specs=in_hbm,
        scratch_shapes=[
            pltpu.VMEM((count, parts, rows // parts, feats), jnp.float32),
            pltpu.SemaphoreType.DMA((count, parts)),
            pltpu.SemaphoreType.DMA((count, parts)),
        ],
        input_output_aliases={} if out is None else {2 + count: 0},
        compiler_params=pltpu.CompilerParams(vmem_limit_bytes=32 * 1024 * 1024),
        cost_estimate=pl.CostEstimate(flops=4 * count * rows * feats, bytes_accessed=8 * count * rows * feats, transcendentals=0),
        name="place",
    )(*args)


def share_moments(told, row_count):
    peers = told.shape[0]
    outer_count = lax.axis_size("outer")
    slots = told[:, 2, 0].astype(jnp.int32)[lane_base(peers) ^ jnp.arange(peers, dtype=jnp.int32)]
    level_count = row_count
    centers, spreads = told[:, 0], told[:, 1]
    while centers.shape[0] > 1:
        centers, spreads = merge_pair(centers[0::2], spreads[0::2], centers[1::2], spreads[1::2], level_count * 0.5)
        level_count *= 2
    pair = jnp.concatenate([centers, spreads], axis=0)
    for bit in range(outer_count.bit_length() - 1):
        other = lax.ppermute(pair, "outer", [(i, i ^ 1 << bit) for i in range(outer_count)])
        center, spread = merge_pair(pair[0], pair[1], other[0], other[1], level_count * 0.5)
        level_count *= 2
        pair = jnp.stack([center, spread])
    center, variance = pair[0], pair[1] / level_count
    return slots, center, variance, jnp.stack([center, lax.rsqrt(variance + eps_value)])


def body(features, dest, slot):
    row_count, _ = features.shape
    peers, outer_count = dest.shape[0], lax.axis_size("outer")
    order = lane_order(peers)
    inverse, first = pick_first(order[:1], dest, features)
    payload, later = pick_rest(order[1:], order[:1], inverse, slot, features)
    picked, got = list(first) + list(later), []

    def send(block, lane):
        pairs = [(o * peers + i, o * peers + (i ^ lane ^ (o & 1) * (peers // 2))) for o in range(outer_count) for i in range(peers)]
        return lax.ppermute(block, ("outer", "inner"), pairs)

    def place_lanes(begin, end, out):
        return place(order[begin:end], got[begin:end], slots, scale, out, row_count, begin >= peers - window)

    out, placed = None, 0
    for j in range(peers):
        if j >= window:
            k = j - window
            values = [picked[j], got[k]]
            if k == 0:
                values.append(payload)
            elif k == window - 1:
                values.append(told)
            elif k > window and k % window == 0:
                out = place_lanes(placed, k, out)
                placed = k
                values.append(out)
            picked[j], got[k], *extra = lax.optimization_barrier(tuple(values))
            if k == 0:
                told = lax.all_to_all(extra[0], "inner", split_axis=0, concat_axis=0, tiled=True)
            elif k == window - 1:
                slots, center, variance, scale = share_moments(extra[0], row_count)
            elif extra:
                out = extra[0]
        got.append(send(picked[j], order[j]))
    for end in (peers - window, peers - window // 2, peers):
        out = place_lanes(placed, end, out)
        placed = end
    return (out, jnp.stack([center, variance]))


def solution(mesh):
    in_specs = (P(("outer", "inner"), None), P(("outer", "inner")), P(("outer", "inner")))
    out_specs = (P(("outer", "inner"), None), P())
    return jax.shard_map(body, mesh=mesh, in_specs=in_specs, out_specs=out_specs, check_vma=False)
```

```python
import functools

import jax
import jax.numpy as jnp
from jax import lax
from jax.experimental import pallas as pl
from jax.experimental.pallas import tpu as pltpu
from jax.sharding import PartitionSpec as P

eps_value = 1e-06
clip_value = 3.0
mark_width = 128
window = 4
head_count = 2
tell_step = 1
told_step = 5
place_steps = (8,)
in_smem, in_vmem = pl.BlockSpec(memory_space=pltpu.SMEM), pl.BlockSpec(memory_space=pltpu.VMEM)
in_hbm, in_any = pl.BlockSpec(memory_space=pltpu.HBM), pl.BlockSpec(memory_space=pl.ANY)


def merge_pair(center_a, spread_a, center_b, spread_b, half):
    gap = center_b - center_a
    return ((center_a + center_b) * 0.5, spread_a + spread_b + gap * gap * half)


def pin(array, space=pltpu.HBM):
    return pltpu.with_memory_space_constraint(array, space)


def lane_order(peers):
    half = peers // 2
    far = list(range(0, half, 2)) + list(range(1, half, 2))
    near = list(range(1, half, 2)) + list(range(2, half, 2)) + [0]
    return [lane for f, n in zip(far, near) for lane in (half + f, n)]


def last_cuts(peers):
    return (peers - 4,)


def lane_base(peers):
    return lax.axis_index("inner") ^ ((lax.axis_index("outer") & 1) * (peers // 2))


def first_kernel(lanes, dest_ref, features_ref, inverse_ref, *rest):
    outs, sems = rest[:-1], rest[-1]
    peers, rows = dest_ref.shape[0], outs[0].shape[0]
    base = lane_base(peers)
    for b in range(peers):
        inverse_ref[dest_ref[b] ^ base] = b
    copies = []
    for i, lane in enumerate(lanes):
        start = pl.multiple_of(inverse_ref[lane] * rows, 8)
        copies.append(pltpu.make_async_copy(features_ref.at[pl.ds(start, rows)], outs[i], sems.at[i]))
        copies[-1].start()
    for copy in copies:
        copy.wait()


def pick_first(lanes, dest, features):
    count, (row_count, feats) = len(lanes), features.shape
    rows = row_count // dest.shape[0]
    res = pl.pallas_call(
        functools.partial(first_kernel, lanes),
        out_shape=[jax.ShapeDtypeStruct(dest.shape, jnp.int32)] + [pltpu.VMEM((rows, feats), features.dtype)] * count,
        in_specs=[in_smem, in_hbm],
        out_specs=[in_smem] + [in_vmem] * count,
        scratch_shapes=[pltpu.SemaphoreType.DMA((count,))],
        name="pick_first",
    )(dest, pin(features))
    return res[0], res[1:]


def rest_kernel(lanes, first, inverse_ref, slot_ref, features_ref, payload_ref, *rest):
    outs, (held, in_sems, out_sems) = rest[: len(lanes)], rest[len(lanes) :]
    peers, rows, feats = held.shape
    base = lane_base(peers)
    order = lanes + first
    fetches = []
    for lane in order:
        start = pl.multiple_of(inverse_ref[lane] * rows, 8)
        fetches.append(pltpu.make_async_copy(features_ref.at[pl.ds(start, rows)], held.at[lane], in_sems.at[lane]))
        fetches[-1].start()

    def fold(x):
        return jnp.sum(x.reshape(rows // 8, 8, feats), axis=0)

    stores, parts = [], []
    for i, lane in enumerate(order):
        fetches[i].wait()
        if i < len(lanes):
            stores.append(pltpu.make_async_copy(held.at[lane], outs[i], out_sems.at[i]))
            stores[-1].start()
        center = jnp.sum(fold(held[lane]), axis=0, keepdims=True) / rows
        gap = held[lane] - center
        parts.append((center, jnp.sum(fold(gap * gap), axis=0, keepdims=True)))
    level_count = rows
    while len(parts) > 1:
        parts = [merge_pair(*parts[i], *parts[i + 1], level_count * 0.5) for i in range(0, len(parts), 2)]
        level_count *= 2
    moments = jnp.concatenate(list(parts[0]), axis=1)
    for lane in range(peers):
        mark = jnp.full((1, mark_width), slot_ref[inverse_ref[lane]].astype(jnp.float32))
        payload_ref[lane ^ base] = jnp.concatenate([moments, mark], axis=1)
    for store in stores:
        store.wait()


def pick_rest(lanes, first, inverse, slot, features):
    peers, (row_count, feats) = inverse.shape[0], features.shape
    rows = row_count // peers
    res = pl.pallas_call(
        functools.partial(rest_kernel, lanes, first),
        out_shape=[jax.ShapeDtypeStruct((peers, 1, 2 * feats + mark_width), jnp.float32)] + [pltpu.HBM((rows, feats), features.dtype)] * len(lanes),
        in_specs=[in_smem, in_smem, in_hbm],
        out_specs=[in_vmem] + [in_hbm] * len(lanes),
        scratch_shapes=[
            pltpu.VMEM((peers, rows, feats), jnp.float32),
            pltpu.SemaphoreType.DMA((peers,)),
            pltpu.SemaphoreType.DMA((len(lanes),)),
        ],
        compiler_params=pltpu.CompilerParams(vmem_limit_bytes=32 * 1024 * 1024),
        cost_estimate=pl.CostEstimate(flops=6 * features.size, bytes_accessed=8 * features.size, transcendentals=0),
        name="pick_rest",
    )(inverse, slot, pin(features))
    return res[0], res[1:]


def place_kernel(lanes, near_by, slot_ref, scale_ref, *rest):
    blocks, (out_ref, held, in_sems, out_sems) = rest[: len(lanes)], rest[-4:]
    _, parts, part_rows, _ = held.shape
    plan = []
    for n, lane in enumerate(lanes):
        start = slot_ref[lane] * (parts * part_rows)
        for i in range(parts):
            target = pl.ds(pl.multiple_of(start + i * part_rows, 8), part_rows)
            source = blocks[n].at[pl.ds(i * part_rows, part_rows)]
            fetch = None if near_by else pltpu.make_async_copy(source, held.at[n, i], in_sems.at[n, i])
            if fetch is not None:
                fetch.start()
            plan.append((n, i, source, fetch, pltpu.make_async_copy(held.at[n, i], out_ref.at[target], out_sems.at[n, i])))
    center, factor = scale_ref[0:1], scale_ref[1:2]
    for n, i, source, fetch, store in plan:
        if fetch is not None:
            fetch.wait()
        values = source[...] if fetch is None else held[n, i]
        held[n, i] = jnp.clip((values - center) * factor, -clip_value, clip_value)
        store.start()
    for *_, store in plan:
        store.wait()


def place(lanes, blocks, slots, scale, out, row_count, near_by):
    rows, feats = blocks[0].shape
    count, parts = len(lanes), max(1, rows // 32)
    space, spec = (pltpu.VMEM, in_vmem) if near_by else (pltpu.HBM, in_hbm)
    args = [slots, scale] + [pin(block, space) for block in blocks] + ([] if out is None else [pin(out)])
    return pl.pallas_call(
        functools.partial(place_kernel, lanes, near_by),
        out_shape=pltpu.HBM((row_count, feats), jnp.float32),
        in_specs=[in_smem, in_vmem] + [spec] * count + ([] if out is None else [in_hbm]),
        out_specs=in_hbm,
        scratch_shapes=[
            pltpu.VMEM((count, parts, rows // parts, feats), jnp.float32),
            pltpu.SemaphoreType.DMA((count, parts)),
            pltpu.SemaphoreType.DMA((count, parts)),
        ],
        input_output_aliases={} if out is None else {2 + count: 0},
        compiler_params=pltpu.CompilerParams(vmem_limit_bytes=32 * 1024 * 1024),
        cost_estimate=pl.CostEstimate(flops=4 * count * rows * feats, bytes_accessed=8 * count * rows * feats, transcendentals=0),
        name="place",
    )(*args)


def share_moments(told, row_count):
    peers, feats = told.shape[0], (told.shape[2] - mark_width) // 2
    outer_count = lax.axis_size("outer")
    slots = told[:, 0, 2 * feats].astype(jnp.int32)[lane_base(peers) ^ jnp.arange(peers, dtype=jnp.int32)]
    level_count = row_count
    centers, spreads = told[:, 0, :feats], told[:, 0, feats : 2 * feats]
    while centers.shape[0] > 1:
        centers, spreads = merge_pair(centers[0::2], spreads[0::2], centers[1::2], spreads[1::2], level_count * 0.5)
        level_count *= 2
    pair = jnp.concatenate([centers, spreads], axis=0)
    for bit in range(outer_count.bit_length() - 1):
        other = lax.ppermute(pair, "outer", [(i, i ^ 1 << bit) for i in range(outer_count)])
        center, spread = merge_pair(pair[0], pair[1], other[0], other[1], level_count * 0.5)
        level_count *= 2
        pair = jnp.stack([center, spread])
    center, variance = pair[0], pair[1] / level_count
    return slots, center, variance, jnp.stack([center, lax.rsqrt(variance + eps_value)])


def body(features, dest, slot):
    row_count, _ = features.shape
    peers, outer_count = dest.shape[0], lax.axis_size("outer")
    order = lane_order(peers)
    inverse, first = pick_first(order[:head_count], dest, features)
    payload, later = pick_rest(order[head_count:], order[:head_count], inverse, slot, features)
    picked, got = list(first) + list(later), []

    def send(block, lane):
        pairs = [(o * peers + i, o * peers + (i ^ lane ^ (o & 1) * (peers // 2))) for o in range(outer_count) for i in range(peers)]
        return lax.ppermute(block, ("outer", "inner"), pairs)

    def place_lanes(begin, end, out, near_by=False):
        return place(order[begin:end], got[begin:end], slots, scale, out, row_count, near_by)

    out, placed = None, 0
    for j in range(peers):
        if j >= window:
            k = j - window
            extra = []
            if k == tell_step:
                extra = [payload]
            elif k == told_step:
                extra = [told]
            elif k in place_steps:
                out = place_lanes(placed, k, out)
                placed = k
                extra = [out]
            picked[j], got[k], *extra = lax.optimization_barrier((picked[j], got[k], *extra))
            if k == tell_step:
                told = lax.all_to_all(extra[0], "inner", split_axis=0, concat_axis=0, tiled=True)
            elif k == told_step:
                slots, center, variance, scale = share_moments(extra[0], row_count)
            elif extra:
                out = extra[0]
        got.append(send(picked[j], order[j]))
    for begin, end in zip((placed,) + last_cuts(peers), last_cuts(peers) + (peers,)):
        out = place_lanes(begin, end, out, begin >= peers - 4)
    return (out, jnp.stack([center, variance]))


def solution(mesh):
    in_specs = (P(("outer", "inner"), None), P(("outer", "inner")), P(("outer", "inner")))
    out_specs = (P(("outer", "inner"), None), P())
    return jax.shard_map(body, mesh=mesh, in_specs=in_specs, out_specs=out_specs, check_vma=False)
```

```python
import functools

import jax
import jax.numpy as jnp
from jax import lax
from jax.experimental import pallas as pl
from jax.experimental.pallas import tpu as pltpu
from jax.sharding import PartitionSpec as P

eps_value = 1e-06
clip_value = 3.0
message_width = 256
window = 4
head_count = 2
tell_step = 1
told_step = 5
share_step = 7
shared_step = 9
place_steps = (10,)
in_smem, in_vmem = pl.BlockSpec(memory_space=pltpu.SMEM), pl.BlockSpec(memory_space=pltpu.VMEM)
in_hbm, in_any = pl.BlockSpec(memory_space=pltpu.HBM), pl.BlockSpec(memory_space=pl.ANY)


def merge_pair(center_a, spread_a, center_b, spread_b, half):
    gap = center_b - center_a
    return ((center_a + center_b) * 0.5, spread_a + spread_b + gap * gap * half)


def pin(array, space=pltpu.HBM):
    return pltpu.with_memory_space_constraint(array, space)


def lane_order(peers):
    half = peers // 2
    far = list(range(0, half, 2)) + list(range(1, half, 2))
    near = list(range(1, half, 2)) + list(range(2, half, 2)) + [0]
    return [lane for f, n in zip(far, near) for lane in (half + f, n)]


def last_cuts(peers):
    return (peers - 4,)


def lane_base(peers):
    return lax.axis_index("inner") ^ ((lax.axis_index("outer") & 1) * (peers // 2))


def invert(dest_ref, inverse):
    peers = dest_ref.shape[0]
    base = lane_base(peers)
    for b in range(peers):
        inverse[dest_ref[b] ^ base] = b
    return base


def first_kernel(lanes, dest_ref, features_ref, *rest):
    outs, (inverse, sems) = rest[:-2], rest[-2:]
    rows, parts = outs[0].shape[0], sems.shape[1]
    invert(dest_ref, inverse)
    copies = []
    for i, lane in enumerate(lanes):
        for p in range(parts):
            start = pl.multiple_of(inverse[lane] * rows + p * (rows // parts), 8)
            target = outs[i].at[pl.ds(p * (rows // parts), rows // parts)]
            copies.append(pltpu.make_async_copy(features_ref.at[pl.ds(start, rows // parts)], target, sems.at[i, p]))
            copies[-1].start()
    for copy in copies:
        copy.wait()


def pick_first(lanes, dest, features):
    count, (row_count, feats) = len(lanes), features.shape
    rows = row_count // dest.shape[0]
    return pl.pallas_call(
        functools.partial(first_kernel, lanes),
        out_shape=[pltpu.VMEM((rows, feats), features.dtype)] * count,
        in_specs=[in_smem, in_hbm],
        out_specs=[in_vmem] * count,
        scratch_shapes=[pltpu.SMEM(dest.shape, jnp.int32), pltpu.SemaphoreType.DMA((count, max(1, rows // 32)))],
        name="pick_first",
    )(dest, pin(features))


def rest_kernel(lanes, first, dest_ref, slot_ref, features_ref, payload_ref, *rest):
    outs, (held, inverse_ref, in_sems, out_sems) = rest[: len(lanes)], rest[len(lanes) :]
    peers, rows, feats = held.shape
    base = invert(dest_ref, inverse_ref)
    order = lanes + first
    fetches = []
    for lane in order:
        start = pl.multiple_of(inverse_ref[lane] * rows, 8)
        fetches.append(pltpu.make_async_copy(features_ref.at[pl.ds(start, rows)], held.at[lane], in_sems.at[lane]))
        fetches[-1].start()

    def fold(x):
        return jnp.sum(x.reshape(rows // 8, 8, feats), axis=0)

    stores, parts = [], []
    for i, lane in enumerate(order):
        fetches[i].wait()
        if i < len(lanes):
            stores.append(pltpu.make_async_copy(held.at[lane], outs[i], out_sems.at[i]))
            stores[-1].start()
        center = jnp.sum(fold(held[lane]), axis=0, keepdims=True) / rows
        gap = held[lane] - center
        parts.append((center, jnp.sum(fold(gap * gap), axis=0, keepdims=True)))
    level_count = rows
    while len(parts) > 1:
        parts = [merge_pair(*parts[i], *parts[i + 1], level_count * 0.5) for i in range(0, len(parts), 2)]
        level_count *= 2
    center, spread = parts[0]
    chunk = feats // peers
    for peer in range(peers):
        mark = jnp.full((1, payload_ref.shape[2] - 2 * chunk), slot_ref[inverse_ref[peer ^ base]].astype(jnp.float32))
        pieces = [x[:, peer * chunk : (peer + 1) * chunk] for x in (center, spread)]
        payload_ref[peer] = jnp.concatenate(pieces + [mark], axis=1)
    for store in stores:
        store.wait()


def pick_rest(lanes, first, dest, slot, features):
    peers, (row_count, feats) = dest.shape[0], features.shape
    rows = row_count // peers
    res = pl.pallas_call(
        functools.partial(rest_kernel, lanes, first),
        out_shape=[jax.ShapeDtypeStruct((peers, 1, message_width), jnp.float32)] + [pltpu.HBM((rows, feats), features.dtype)] * len(lanes),
        in_specs=[in_smem, in_smem, in_hbm],
        out_specs=[in_vmem] + [in_hbm] * len(lanes),
        scratch_shapes=[
            pltpu.VMEM((peers, rows, feats), jnp.float32),
            pltpu.SMEM((peers,), jnp.int32),
            pltpu.SemaphoreType.DMA((peers,)),
            pltpu.SemaphoreType.DMA((len(lanes),)),
        ],
        compiler_params=pltpu.CompilerParams(vmem_limit_bytes=32 * 1024 * 1024),
        cost_estimate=pl.CostEstimate(flops=6 * features.size, bytes_accessed=8 * features.size, transcendentals=0),
        name="pick_rest",
    )(dest, slot, pin(features))
    return res[0], res[1:]


def place_kernel(lanes, near_by, slot_ref, scale_ref, *rest):
    blocks, (out_ref, held, in_sems, out_sems) = rest[: len(lanes)], rest[-4:]
    _, parts, part_rows, _ = held.shape
    plan = []
    for n, lane in enumerate(lanes):
        start = slot_ref[lane] * (parts * part_rows)
        for i in range(parts):
            target = pl.ds(pl.multiple_of(start + i * part_rows, 8), part_rows)
            source = blocks[n].at[pl.ds(i * part_rows, part_rows)]
            fetch = None if near_by else pltpu.make_async_copy(source, held.at[n, i], in_sems.at[n, i])
            if fetch is not None:
                fetch.start()
            plan.append((n, i, source, fetch, pltpu.make_async_copy(held.at[n, i], out_ref.at[target], out_sems.at[n, i])))
    center, factor = scale_ref[0:1], scale_ref[1:2]
    for n, i, source, fetch, store in plan:
        if fetch is not None:
            fetch.wait()
        values = source[...] if fetch is None else held[n, i]
        held[n, i] = jnp.clip((values - center) * factor, -clip_value, clip_value)
        store.start()
    for *_, store in plan:
        store.wait()


def place(lanes, blocks, slots, scale, out, row_count, near_by):
    rows, feats = blocks[0].shape
    count, parts = len(lanes), max(1, rows // 32)
    space, spec = (pltpu.VMEM, in_vmem) if near_by else (pltpu.HBM, in_hbm)
    args = [slots, scale] + [pin(block, space) for block in blocks] + ([] if out is None else [pin(out)])
    return pl.pallas_call(
        functools.partial(place_kernel, lanes, near_by),
        out_shape=pltpu.HBM((row_count, feats), jnp.float32),
        in_specs=[in_smem, in_vmem] + [spec] * count + ([] if out is None else [in_hbm]),
        out_specs=in_hbm,
        scratch_shapes=[
            pltpu.VMEM((count, parts, rows // parts, feats), jnp.float32),
            pltpu.SemaphoreType.DMA((count, parts)),
            pltpu.SemaphoreType.DMA((count, parts)),
        ],
        input_output_aliases={} if out is None else {2 + count: 0},
        compiler_params=pltpu.CompilerParams(vmem_limit_bytes=32 * 1024 * 1024),
        cost_estimate=pl.CostEstimate(flops=4 * count * rows * feats, bytes_accessed=8 * count * rows * feats, transcendentals=0),
        name="place",
    )(*args)


def merge_chunk(told, row_count, feats):
    peers, outer_count = told.shape[0], lax.axis_size("outer")
    chunk = feats // peers
    slots = told[:, 0, 2 * chunk].astype(jnp.int32)[lane_base(peers) ^ jnp.arange(peers, dtype=jnp.int32)]
    level_count = row_count
    centers, spreads = told[:, 0, :chunk], told[:, 0, chunk : 2 * chunk]
    while centers.shape[0] > 1:
        centers, spreads = merge_pair(centers[0::2], spreads[0::2], centers[1::2], spreads[1::2], level_count * 0.5)
        level_count *= 2
    pair = jnp.concatenate([centers, spreads], axis=0)
    for bit in range(outer_count.bit_length() - 1):
        other = lax.ppermute(pair, "outer", [(i, i ^ 1 << bit) for i in range(outer_count)])
        center, spread = merge_pair(pair[0], pair[1], other[0], other[1], level_count * 0.5)
        level_count *= 2
        pair = jnp.stack([center, spread])
    return slots, jnp.broadcast_to(pair.reshape(1, 1, 2 * chunk), (peers, 1, 2 * chunk))


def spread_moments(shares, total_rows):
    chunk = shares.shape[2] // 2
    center, variance = shares[:, 0, :chunk].reshape(-1), shares[:, 0, chunk:].reshape(-1) / total_rows
    return center, variance, jnp.stack([center, lax.rsqrt(variance + eps_value)])


def body(features, dest, slot):
    row_count, feats = features.shape
    peers, outer_count = dest.shape[0], lax.axis_size("outer")
    order = lane_order(peers)
    first = pick_first(order[:head_count], dest, features)
    dest, slot, *first = lax.optimization_barrier((dest, slot, *first))
    payload, later = pick_rest(order[head_count:], order[:head_count], dest, slot, features)
    picked, got = list(first) + list(later), []

    def send(block, lane):
        pairs = [(o * peers + i, o * peers + (i ^ lane ^ (o & 1) * (peers // 2))) for o in range(outer_count) for i in range(peers)]
        return lax.ppermute(block, ("outer", "inner"), pairs)

    def place_lanes(begin, end, out, near_by=False):
        return place(order[begin:end], got[begin:end], slots, scale, out, row_count, near_by)

    out, placed = None, 0
    for j in range(peers):
        if j >= window:
            k = j - window
            extra = []
            if k == tell_step:
                extra = [payload]
            elif k == told_step:
                extra = [told]
            elif k == share_step:
                extra = [share]
            elif k == shared_step:
                extra = [shared]
            elif k in place_steps:
                out = place_lanes(placed, k, out)
                placed = k
                extra = [out]
            picked[j], got[k], *extra = lax.optimization_barrier((picked[j], got[k], *extra))
            if k == tell_step:
                told = lax.all_to_all(extra[0], "inner", split_axis=0, concat_axis=0, tiled=True)
            elif k == told_step:
                slots, share = merge_chunk(extra[0], row_count, feats)
            elif k == share_step:
                shared = lax.all_to_all(extra[0], "inner", split_axis=0, concat_axis=0, tiled=True)
            elif k == shared_step:
                center, variance, scale = spread_moments(extra[0], row_count * peers * outer_count)
            elif extra:
                out = extra[0]
        got.append(send(picked[j], order[j]))
    for begin, end in zip((placed,) + last_cuts(peers), last_cuts(peers) + (peers,)):
        out = place_lanes(begin, end, out, begin >= peers - 4)
    return (out, jnp.stack([center, variance]))


def solution(mesh):
    in_specs = (P(("outer", "inner"), None), P(("outer", "inner")), P(("outer", "inner")))
    out_specs = (P(("outer", "inner"), None), P())
    return jax.shard_map(body, mesh=mesh, in_specs=in_specs, out_specs=out_specs, check_vma=False)
```

```python
import functools

import jax
import jax.numpy as jnp
from jax import lax
from jax.experimental import pallas as pl
from jax.experimental.pallas import tpu as pltpu
from jax.sharding import PartitionSpec as P

eps_value = 1e-06
clip_value = 3.0
message_width = 256
window = 4
head_count = 2
tell_step = 1
told_step = 5
share_step = 7
shared_step = 9
place_steps = (10,)
in_smem, in_vmem = pl.BlockSpec(memory_space=pltpu.SMEM), pl.BlockSpec(memory_space=pltpu.VMEM)
in_hbm, in_any = pl.BlockSpec(memory_space=pltpu.HBM), pl.BlockSpec(memory_space=pl.ANY)


def merge_pair(center_a, spread_a, center_b, spread_b, half):
    gap = center_b - center_a
    return ((center_a + center_b) * 0.5, spread_a + spread_b + gap * gap * half)


def pin(array, space=pltpu.HBM):
    return pltpu.with_memory_space_constraint(array, space)


def lane_order(peers):
    half = peers // 2
    far = list(range(0, half, 2)) + list(range(1, half, 2))
    near = list(range(1, half, 2)) + list(range(2, half, 2)) + [0]
    return [lane for f, n in zip(far, near) for lane in (half + f, n)]


def last_cuts(peers):
    return (peers - 4, peers - 2)


def lane_base(peers):
    return lax.axis_index("inner") ^ ((lax.axis_index("outer") & 1) * (peers // 2))


def invert(dest_ref, inverse):
    peers = dest_ref.shape[0]
    base = lane_base(peers)
    for b in range(peers):
        inverse[dest_ref[b] ^ base] = b
    return base


def first_kernel(lanes, dest_ref, features_ref, *rest):
    outs, (inverse, sems) = rest[:-2], rest[-2:]
    rows, parts = outs[0].shape[0], sems.shape[1]
    invert(dest_ref, inverse)
    copies = []
    for i, lane in enumerate(lanes):
        for p in range(parts):
            start = pl.multiple_of(inverse[lane] * rows + p * (rows // parts), 8)
            target = outs[i].at[pl.ds(p * (rows // parts), rows // parts)]
            copies.append(pltpu.make_async_copy(features_ref.at[pl.ds(start, rows // parts)], target, sems.at[i, p]))
            copies[-1].start()
    for copy in copies:
        copy.wait()


def pick_first(lanes, dest, features):
    count, (row_count, feats) = len(lanes), features.shape
    rows = row_count // dest.shape[0]
    return pl.pallas_call(
        functools.partial(first_kernel, lanes),
        out_shape=[pltpu.VMEM((rows, feats), features.dtype)] * count,
        in_specs=[in_smem, in_hbm],
        out_specs=[in_vmem] * count,
        scratch_shapes=[pltpu.SMEM(dest.shape, jnp.int32), pltpu.SemaphoreType.DMA((count, 1))],
        name="pick_first",
    )(dest, pin(features))


def rest_kernel(lanes, first, dest_ref, slot_ref, features_ref, payload_ref, *rest):
    outs, (held, inverse_ref, in_sems, out_sems) = rest[: len(lanes)], rest[len(lanes) :]
    peers, rows, feats = held.shape
    base = invert(dest_ref, inverse_ref)
    order = lanes + first
    fetches = []
    for lane in order:
        start = pl.multiple_of(inverse_ref[lane] * rows, 8)
        fetches.append(pltpu.make_async_copy(features_ref.at[pl.ds(start, rows)], held.at[lane], in_sems.at[lane]))
        fetches[-1].start()

    def fold(x):
        return jnp.sum(x.reshape(rows // 8, 8, feats), axis=0)

    stores, parts = [], []
    for i, lane in enumerate(order):
        fetches[i].wait()
        if i < len(lanes):
            stores.append(pltpu.make_async_copy(held.at[lane], outs[i], out_sems.at[i]))
            stores[-1].start()
        center = jnp.sum(fold(held[lane]), axis=0, keepdims=True) / rows
        gap = held[lane] - center
        parts.append((center, jnp.sum(fold(gap * gap), axis=0, keepdims=True)))
    level_count = rows
    while len(parts) > 1:
        parts = [merge_pair(*parts[i], *parts[i + 1], level_count * 0.5) for i in range(0, len(parts), 2)]
        level_count *= 2
    center, spread = parts[0]
    chunk = feats // peers
    for peer in range(peers):
        mark = jnp.full((1, payload_ref.shape[2] - 2 * chunk), slot_ref[inverse_ref[peer ^ base]].astype(jnp.float32))
        pieces = [x[:, peer * chunk : (peer + 1) * chunk] for x in (center, spread)]
        payload_ref[peer] = jnp.concatenate(pieces + [mark], axis=1)
    for store in stores:
        store.wait()


def pick_rest(lanes, first, dest, slot, features):
    peers, (row_count, feats) = dest.shape[0], features.shape
    rows = row_count // peers
    res = pl.pallas_call(
        functools.partial(rest_kernel, lanes, first),
        out_shape=[jax.ShapeDtypeStruct((peers, 1, message_width), jnp.float32)] + [pltpu.HBM((rows, feats), features.dtype)] * len(lanes),
        in_specs=[in_smem, in_smem, in_hbm],
        out_specs=[in_vmem] + [in_hbm] * len(lanes),
        scratch_shapes=[
            pltpu.VMEM((peers, rows, feats), jnp.float32),
            pltpu.SMEM((peers,), jnp.int32),
            pltpu.SemaphoreType.DMA((peers,)),
            pltpu.SemaphoreType.DMA((len(lanes),)),
        ],
        compiler_params=pltpu.CompilerParams(vmem_limit_bytes=32 * 1024 * 1024),
        cost_estimate=pl.CostEstimate(flops=6 * features.size, bytes_accessed=8 * features.size, transcendentals=0),
        name="pick_rest",
    )(dest, slot, pin(features))
    return res[0], res[1:]


def place_kernel(lanes, near_by, slot_ref, scale_ref, *rest):
    blocks, (out_ref, held, in_sems, out_sems) = rest[: len(lanes)], rest[-4:]
    _, parts, part_rows, _ = held.shape
    plan = []
    for n, lane in enumerate(lanes):
        start = jnp.max(slot_ref[lane : lane + 1, :]) * (parts * part_rows)
        for i in range(parts):
            target = pl.ds(pl.multiple_of(start + i * part_rows, 8), part_rows)
            source = blocks[n].at[pl.ds(i * part_rows, part_rows)]
            fetch = None if near_by else pltpu.make_async_copy(source, held.at[n, i], in_sems.at[n, i])
            if fetch is not None:
                fetch.start()
            plan.append((n, i, source, fetch, pltpu.make_async_copy(held.at[n, i], out_ref.at[target], out_sems.at[n, i])))
    center, factor = scale_ref[0:1], scale_ref[1:2]
    for n, i, source, fetch, store in plan:
        if fetch is not None:
            fetch.wait()
        values = source[...] if fetch is None else held[n, i]
        held[n, i] = jnp.clip((values - center) * factor, -clip_value, clip_value)
        store.start()
    for *_, store in plan:
        store.wait()


def place(lanes, blocks, slots, scale, out, row_count, near_by):
    rows, feats = blocks[0].shape
    count, parts = len(lanes), max(1, rows // 32)
    space, spec = (pltpu.VMEM, in_vmem) if near_by else (pltpu.HBM, in_hbm)
    args = [pin(slots, pltpu.VMEM), pin(scale, pltpu.VMEM)] + [pin(block, space) for block in blocks] + ([] if out is None else [pin(out)])
    return pl.pallas_call(
        functools.partial(place_kernel, lanes, near_by),
        out_shape=pltpu.HBM((row_count, feats), jnp.float32),
        in_specs=[in_vmem, in_vmem] + [spec] * count + ([] if out is None else [in_hbm]),
        out_specs=in_hbm,
        scratch_shapes=[
            pltpu.VMEM((count, parts, rows // parts, feats), jnp.float32),
            pltpu.SemaphoreType.DMA((count, parts)),
            pltpu.SemaphoreType.DMA((count, parts)),
        ],
        input_output_aliases={} if out is None else {2 + count: 0},
        compiler_params=pltpu.CompilerParams(vmem_limit_bytes=32 * 1024 * 1024),
        cost_estimate=pl.CostEstimate(flops=4 * count * rows * feats, bytes_accessed=8 * count * rows * feats, transcendentals=0),
        name="place",
    )(*args)


def merge_chunk(told, row_count, feats):
    peers, outer_count = told.shape[0], lax.axis_size("outer")
    chunk = feats // peers
    slots = told[:, 0, message_width - 128 :].astype(jnp.int32)[lane_base(peers) ^ jnp.arange(peers, dtype=jnp.int32)]
    level_count = row_count
    centers, spreads = told[:, 0, :chunk], told[:, 0, chunk : 2 * chunk]
    while centers.shape[0] > 1:
        centers, spreads = merge_pair(centers[0::2], spreads[0::2], centers[1::2], spreads[1::2], level_count * 0.5)
        level_count *= 2
    pair = jnp.concatenate([centers, spreads], axis=0)
    for bit in range(outer_count.bit_length() - 1):
        other = lax.ppermute(pair, "outer", [(i, i ^ 1 << bit) for i in range(outer_count)])
        center, spread = merge_pair(pair[0], pair[1], other[0], other[1], level_count * 0.5)
        level_count *= 2
        pair = jnp.stack([center, spread])
    return slots, jnp.broadcast_to(pair.reshape(1, 1, 2 * chunk), (peers, 1, 2 * chunk))


def spread_moments(shares, total_rows):
    chunk = shares.shape[2] // 2
    center, variance = shares[:, 0, :chunk].reshape(-1), shares[:, 0, chunk:].reshape(-1) / total_rows
    return center, variance, jnp.stack([center, lax.rsqrt(variance + eps_value)])


def body(features, dest, slot):
    row_count, feats = features.shape
    peers, outer_count = dest.shape[0], lax.axis_size("outer")
    order = lane_order(peers)
    first = pick_first(order[:head_count], dest, features)
    dest, slot, *first = lax.optimization_barrier((dest, slot, *first))
    payload, later = pick_rest(order[head_count:], order[:head_count], dest, slot, features)
    picked, got = list(first) + list(later), []

    def send(block, lane):
        pairs = [(o * peers + i, o * peers + (i ^ lane ^ (o & 1) * (peers // 2))) for o in range(outer_count) for i in range(peers)]
        return lax.ppermute(block, ("outer", "inner"), pairs)

    def place_lanes(begin, end, out, near_by=False):
        return place(order[begin:end], got[begin:end], slots, scale, out, row_count, near_by)

    out, placed = None, 0
    for j in range(peers):
        if j >= window:
            k = j - window
            extra = []
            if k == tell_step:
                extra = [payload]
            elif k == told_step:
                extra = [told]
            elif k == share_step:
                extra = [share]
            elif k == shared_step:
                extra = [shared]
            elif k in place_steps:
                out = place_lanes(placed, k, out)
                placed = k
                extra = [out]
            picked[j], got[k], *extra = lax.optimization_barrier((picked[j], got[k], *extra))
            if k == tell_step:
                told = lax.all_to_all(extra[0], "inner", split_axis=0, concat_axis=0, tiled=True)
            elif k == told_step:
                slots, share = merge_chunk(extra[0], row_count, feats)
            elif k == share_step:
                shared = lax.all_to_all(extra[0], "inner", split_axis=0, concat_axis=0, tiled=True)
            elif k == shared_step:
                center, variance, scale = spread_moments(extra[0], row_count * peers * outer_count)
            elif extra:
                out = extra[0]
        got.append(send(picked[j], order[j]))
    for begin, end in zip((placed,) + last_cuts(peers), last_cuts(peers) + (peers,)):
        out = place_lanes(begin, end, out, begin >= peers - 4)
    return (out, jnp.stack([center, variance]))


def solution(mesh):
    in_specs = (P(("outer", "inner"), None), P(("outer", "inner")), P(("outer", "inner")))
    out_specs = (P(("outer", "inner"), None), P())
    return jax.shard_map(body, mesh=mesh, in_specs=in_specs, out_specs=out_specs, check_vma=False)
```

```python
import functools

import jax
import jax.numpy as jnp
from jax import lax
from jax.experimental import pallas as pl
from jax.experimental.pallas import tpu as pltpu
from jax.sharding import PartitionSpec as P

eps_value = 1e-06
clip_value = 3.0
message_width = 256
window = 4
head_count = 2
tell_step = 1
told_step = 5
share_step = 7
shared_step = 9
place_steps = (10,)
in_smem, in_vmem = pl.BlockSpec(memory_space=pltpu.SMEM), pl.BlockSpec(memory_space=pltpu.VMEM)
in_hbm, in_any = pl.BlockSpec(memory_space=pltpu.HBM), pl.BlockSpec(memory_space=pl.ANY)


def merge_pair(center_a, spread_a, center_b, spread_b, half):
    gap = center_b - center_a
    return ((center_a + center_b) * 0.5, spread_a + spread_b + gap * gap * half)


def pin(array, space=pltpu.HBM):
    return pltpu.with_memory_space_constraint(array, space)


def lane_order(peers):
    half, quarter = peers // 2, peers // 4
    far = [half + k for k in (*range(0, half, 2), *range(1, half, 2))]
    far[-2:] = far[:-3:-1]
    near = [*range(1, half, 2), *range(2, half, 2), 0]
    at = near.index(quarter)
    near[0], near[at] = quarter, near[0]
    return [lane for pair in zip(far, near) for lane in pair]


def last_cuts(peers):
    return (peers - 4, peers - 2)


def lane_base(peers):
    return lax.axis_index("inner") ^ ((lax.axis_index("outer") & 1) * (peers // 2))


def invert(dest_ref, inverse):
    peers = dest_ref.shape[0]
    base = lane_base(peers)
    for b in range(peers):
        inverse[dest_ref[b] ^ base] = b
    return base


def first_kernel(lanes, dest_ref, features_ref, *rest):
    outs, (inverse, sems) = rest[:-2], rest[-2:]
    rows, parts = outs[0].shape[0], sems.shape[1]
    invert(dest_ref, inverse)
    copies = []
    for i, lane in enumerate(lanes):
        for p in range(parts):
            start = pl.multiple_of(inverse[lane] * rows + p * (rows // parts), 8)
            target = outs[i].at[pl.ds(p * (rows // parts), rows // parts)]
            copies.append(pltpu.make_async_copy(features_ref.at[pl.ds(start, rows // parts)], target, sems.at[i, p]))
            copies[-1].start()
    for copy in copies:
        copy.wait()


def pick_first(lanes, dest, features):
    count, (row_count, feats) = len(lanes), features.shape
    rows = row_count // dest.shape[0]
    return pl.pallas_call(
        functools.partial(first_kernel, lanes),
        out_shape=[pltpu.VMEM((rows, feats), features.dtype)] * count,
        in_specs=[in_smem, in_hbm],
        out_specs=[in_vmem] * count,
        scratch_shapes=[pltpu.SMEM(dest.shape, jnp.int32), pltpu.SemaphoreType.DMA((count, 1))],
        name="pick_first",
    )(dest, pin(features))


def rest_kernel(lanes, first, dest_ref, slot_ref, features_ref, payload_ref, *rest):
    outs, (held, inverse_ref, in_sems, out_sems) = rest[: len(lanes)], rest[len(lanes) :]
    peers, rows, feats = held.shape
    base = invert(dest_ref, inverse_ref)
    order = lanes + first
    fetches = []
    for lane in order:
        start = pl.multiple_of(inverse_ref[lane] * rows, 8)
        fetches.append(pltpu.make_async_copy(features_ref.at[pl.ds(start, rows)], held.at[lane], in_sems.at[lane]))
        fetches[-1].start()

    def fold(x):
        return jnp.sum(x.reshape(rows // 8, 8, feats), axis=0)

    stores, parts = [], []
    for i, lane in enumerate(order):
        fetches[i].wait()
        if i < len(lanes):
            stores.append(pltpu.make_async_copy(held.at[lane], outs[i], out_sems.at[i]))
            stores[-1].start()
        center = jnp.sum(fold(held[lane]), axis=0, keepdims=True) / rows
        gap = held[lane] - center
        parts.append((center, jnp.sum(fold(gap * gap), axis=0, keepdims=True)))
    level_count = rows
    while len(parts) > 1:
        parts = [merge_pair(*parts[i], *parts[i + 1], level_count * 0.5) for i in range(0, len(parts), 2)]
        level_count *= 2
    center, spread = parts[0]
    chunk = feats // peers
    for peer in range(peers):
        mark = jnp.full((1, payload_ref.shape[2] - 2 * chunk), slot_ref[inverse_ref[peer ^ base]].astype(jnp.float32))
        pieces = [x[:, peer * chunk : (peer + 1) * chunk] for x in (center, spread)]
        payload_ref[peer] = jnp.concatenate(pieces + [mark], axis=1)
    for store in stores:
        store.wait()


def pick_rest(lanes, first, dest, slot, features):
    peers, (row_count, feats) = dest.shape[0], features.shape
    rows = row_count // peers
    res = pl.pallas_call(
        functools.partial(rest_kernel, lanes, first),
        out_shape=[jax.ShapeDtypeStruct((peers, 1, message_width), jnp.float32)] + [pltpu.HBM((rows, feats), features.dtype)] * len(lanes),
        in_specs=[in_smem, in_smem, in_hbm],
        out_specs=[in_vmem] + [in_hbm] * len(lanes),
        scratch_shapes=[
            pltpu.VMEM((peers, rows, feats), jnp.float32),
            pltpu.SMEM((peers,), jnp.int32),
            pltpu.SemaphoreType.DMA((peers,)),
            pltpu.SemaphoreType.DMA((len(lanes),)),
        ],
        compiler_params=pltpu.CompilerParams(vmem_limit_bytes=32 * 1024 * 1024),
        cost_estimate=pl.CostEstimate(flops=6 * features.size, bytes_accessed=8 * features.size, transcendentals=0),
        name="pick_rest",
    )(dest, slot, pin(features))
    return res[0], res[1:]


def place_kernel(lanes, near_by, slot_ref, scale_ref, *rest):
    blocks, (out_ref, held, in_sems, out_sems) = rest[: len(lanes)], rest[-4:]
    _, parts, part_rows, _ = held.shape
    plan = []
    for n, lane in enumerate(lanes):
        start = jnp.max(slot_ref[lane : lane + 1, :]) * (parts * part_rows)
        for i in range(parts):
            target = pl.ds(pl.multiple_of(start + i * part_rows, 8), part_rows)
            source = blocks[n].at[pl.ds(i * part_rows, part_rows)]
            fetch = None if near_by else pltpu.make_async_copy(source, held.at[n, i], in_sems.at[n, i])
            if fetch is not None:
                fetch.start()
            plan.append((n, i, source, fetch, pltpu.make_async_copy(held.at[n, i], out_ref.at[target], out_sems.at[n, i])))
    center, factor = scale_ref[0:1], scale_ref[1:2]
    for n, i, source, fetch, store in plan:
        if fetch is not None:
            fetch.wait()
        values = source[...] if fetch is None else held[n, i]
        held[n, i] = jnp.clip((values - center) * factor, -clip_value, clip_value)
        store.start()
    for *_, store in plan:
        store.wait()


def place(lanes, blocks, slots, scale, out, row_count, near_by):
    rows, feats = blocks[0].shape
    count, parts = len(lanes), max(1, rows // 32)
    space, spec = (pltpu.VMEM, in_vmem) if near_by else (pltpu.HBM, in_hbm)
    args = [pin(slots, pltpu.VMEM), pin(scale, pltpu.VMEM)] + [pin(block, space) for block in blocks] + ([] if out is None else [pin(out)])
    return pl.pallas_call(
        functools.partial(place_kernel, lanes, near_by),
        out_shape=pltpu.HBM((row_count, feats), jnp.float32),
        in_specs=[in_vmem, in_vmem] + [spec] * count + ([] if out is None else [in_hbm]),
        out_specs=in_hbm,
        scratch_shapes=[
            pltpu.VMEM((count, parts, rows // parts, feats), jnp.float32),
            pltpu.SemaphoreType.DMA((count, parts)),
            pltpu.SemaphoreType.DMA((count, parts)),
        ],
        input_output_aliases={} if out is None else {2 + count: 0},
        compiler_params=pltpu.CompilerParams(vmem_limit_bytes=32 * 1024 * 1024),
        cost_estimate=pl.CostEstimate(flops=4 * count * rows * feats, bytes_accessed=8 * count * rows * feats, transcendentals=0),
        name="place",
    )(*args)


def merge_chunk(told, row_count, feats):
    peers, outer_count = told.shape[0], lax.axis_size("outer")
    chunk = feats // peers
    slots = told[:, 0, message_width - 128 :].astype(jnp.int32)[lane_base(peers) ^ jnp.arange(peers, dtype=jnp.int32)]
    level_count = row_count
    centers, spreads = told[:, 0, :chunk], told[:, 0, chunk : 2 * chunk]
    while centers.shape[0] > 1:
        centers, spreads = merge_pair(centers[0::2], spreads[0::2], centers[1::2], spreads[1::2], level_count * 0.5)
        level_count *= 2
    pair = jnp.concatenate([centers, spreads], axis=0)
    for bit in range(outer_count.bit_length() - 1):
        other = lax.ppermute(pair, "outer", [(i, i ^ 1 << bit) for i in range(outer_count)])
        center, spread = merge_pair(pair[0], pair[1], other[0], other[1], level_count * 0.5)
        level_count *= 2
        pair = jnp.stack([center, spread])
    return slots, jnp.broadcast_to(pair.reshape(1, 1, 2 * chunk), (peers, 1, 2 * chunk))


def spread_moments(shares, total_rows):
    chunk = shares.shape[2] // 2
    center, variance = shares[:, 0, :chunk].reshape(-1), shares[:, 0, chunk:].reshape(-1) / total_rows
    return center, variance, jnp.stack([center, lax.rsqrt(variance + eps_value)])


def body(features, dest, slot):
    row_count, feats = features.shape
    peers, outer_count = dest.shape[0], lax.axis_size("outer")
    order = lane_order(peers)
    first = pick_first(order[:head_count], dest, features)
    dest, slot, *first = lax.optimization_barrier((dest, slot, *first))
    payload, later = pick_rest(order[head_count:], order[:head_count], dest, slot, features)
    picked, got = list(first) + list(later), []

    def send(block, lane):
        pairs = [(o * peers + i, o * peers + (i ^ lane ^ (o & 1) * (peers // 2))) for o in range(outer_count) for i in range(peers)]
        return lax.ppermute(block, ("outer", "inner"), pairs)

    def place_lanes(begin, end, out, near_by=False):
        return place(order[begin:end], got[begin:end], slots, scale, out, row_count, near_by)

    out, placed = None, 0
    for j in range(peers):
        if j >= window:
            k = j - window
            extra = []
            if k == tell_step:
                extra = [payload]
            elif k == told_step:
                extra = [told]
            elif k == share_step:
                extra = [share]
            elif k == shared_step:
                extra = [shared]
            elif k in place_steps:
                out = place_lanes(placed, k, out)
                placed = k
                extra = [out]
            picked[j], got[k], *extra = lax.optimization_barrier((picked[j], got[k], *extra))
            if k == tell_step:
                told = lax.all_to_all(extra[0], "inner", split_axis=0, concat_axis=0, tiled=True)
            elif k == told_step:
                slots, share = merge_chunk(extra[0], row_count, feats)
            elif k == share_step:
                shared = lax.all_to_all(extra[0], "inner", split_axis=0, concat_axis=0, tiled=True)
            elif k == shared_step:
                center, variance, scale = spread_moments(extra[0], row_count * peers * outer_count)
            elif extra:
                out = extra[0]
        got.append(send(picked[j], order[j]))
    for begin, end in zip((placed,) + last_cuts(peers), last_cuts(peers) + (peers,)):
        out = place_lanes(begin, end, out, begin >= peers - 4)
    return (out, jnp.stack([center, variance]))


def solution(mesh):
    in_specs = (P(("outer", "inner"), None), P(("outer", "inner")), P(("outer", "inner")))
    out_specs = (P(("outer", "inner"), None), P())
    return jax.shard_map(body, mesh=mesh, in_specs=in_specs, out_specs=out_specs, check_vma=False)
```

```python
import functools

import jax
import jax.numpy as jnp
from jax import lax
from jax.experimental import pallas as pl
from jax.experimental.pallas import tpu as pltpu
from jax.sharding import PartitionSpec as P

eps_value = 1e-06
clip_value = 3.0
message_width = 256
window = 4
head_count = 2
tell_step = 1
told_step = 5
share_step = 7
shared_step = 9
place_steps = (10,)
in_smem, in_vmem = pl.BlockSpec(memory_space=pltpu.SMEM), pl.BlockSpec(memory_space=pltpu.VMEM)
in_hbm, in_any = pl.BlockSpec(memory_space=pltpu.HBM), pl.BlockSpec(memory_space=pl.ANY)


def merge_pair(center_a, spread_a, center_b, spread_b, half):
    gap = center_b - center_a
    return ((center_a + center_b) * 0.5, spread_a + spread_b + gap * gap * half)


def pin(array, space=pltpu.HBM):
    return pltpu.with_memory_space_constraint(array, space)


def lane_order(peers):
    half, quarter = peers // 2, peers // 4
    far = [half + k for k in (*range(0, half, 2), *range(1, half, 2))]
    far[-2:] = far[:-3:-1]
    near = [*range(1, half, 2), *range(2, half, 2), 0]
    at = near.index(quarter)
    near[0], near[at] = quarter, near[0]
    return [lane for pair in zip(far, near) for lane in pair]


def last_cuts(peers):
    return (peers - 4, peers - 2)


def lane_base(peers):
    return lax.axis_index("inner") ^ ((lax.axis_index("outer") & 1) * (peers // 2))


def invert(dest_ref, inverse):
    peers = dest_ref.shape[0]
    base = lane_base(peers)
    for b in range(peers):
        inverse[dest_ref[b] ^ base] = b
    return base


def first_kernel(lanes, dest_ref, features_ref, *rest):
    outs, (inverse, sems) = rest[:-2], rest[-2:]
    rows, parts = outs[0].shape[0], sems.shape[1]
    invert(dest_ref, inverse)
    copies = []
    for i, lane in enumerate(lanes):
        for p in range(parts):
            start = pl.multiple_of(inverse[lane] * rows + p * (rows // parts), 8)
            target = outs[i].at[pl.ds(p * (rows // parts), rows // parts)]
            copies.append(pltpu.make_async_copy(features_ref.at[pl.ds(start, rows // parts)], target, sems.at[i, p]))
            copies[-1].start()
    for copy in copies:
        copy.wait()


def pick_first(lanes, dest, features):
    count, (row_count, feats) = len(lanes), features.shape
    rows = row_count // dest.shape[0]
    return pl.pallas_call(
        functools.partial(first_kernel, lanes),
        out_shape=[pltpu.VMEM((rows, feats), features.dtype)] * count,
        in_specs=[in_smem, in_hbm],
        out_specs=[in_vmem] * count,
        scratch_shapes=[pltpu.SMEM(dest.shape, jnp.int32), pltpu.SemaphoreType.DMA((count, 1))],
        name="pick_first",
    )(dest, pin(features))


def rest_kernel(lanes, first, dest_ref, slot_ref, features_ref, payload_ref, *rest):
    outs, (held, inverse_ref, in_sems, out_sems) = rest[: len(lanes)], rest[len(lanes) :]
    peers, rows, feats = held.shape
    base = invert(dest_ref, inverse_ref)
    order = lanes + first
    fetches = []
    for lane in order:
        start = pl.multiple_of(inverse_ref[lane] * rows, 8)
        fetches.append(pltpu.make_async_copy(features_ref.at[pl.ds(start, rows)], held.at[lane], in_sems.at[lane]))
        fetches[-1].start()

    def fold(x):
        return jnp.sum(x.reshape(rows // 8, 8, feats), axis=0)

    stores, parts = [], []
    for i, lane in enumerate(order):
        fetches[i].wait()
        if i < len(lanes):
            stores.append(pltpu.make_async_copy(held.at[lane], outs[i], out_sems.at[i]))
            stores[-1].start()
        center = jnp.sum(fold(held[lane]), axis=0, keepdims=True) / rows
        gap = held[lane] - center
        parts.append((center, jnp.sum(fold(gap * gap), axis=0, keepdims=True)))
    level_count = rows
    while len(parts) > 1:
        parts = [merge_pair(*parts[i], *parts[i + 1], level_count * 0.5) for i in range(0, len(parts), 2)]
        level_count *= 2
    center, spread = parts[0]
    chunk = feats // peers
    for peer in range(peers):
        mark = jnp.full((1, payload_ref.shape[2] - 2 * chunk), slot_ref[inverse_ref[peer ^ base]].astype(jnp.float32))
        pieces = [x[:, peer * chunk : (peer + 1) * chunk] for x in (center, spread)]
        payload_ref[peer] = jnp.concatenate(pieces + [mark], axis=1)
    for store in stores:
        store.wait()


def pick_rest(lanes, first, dest, slot, features):
    peers, (row_count, feats) = dest.shape[0], features.shape
    rows = row_count // peers
    res = pl.pallas_call(
        functools.partial(rest_kernel, lanes, first),
        out_shape=[jax.ShapeDtypeStruct((peers, 1, message_width), jnp.float32)] + [pltpu.HBM((rows, feats), features.dtype)] * len(lanes),
        in_specs=[in_smem, in_smem, in_hbm],
        out_specs=[in_vmem] + [in_hbm] * len(lanes),
        scratch_shapes=[
            pltpu.VMEM((peers, rows, feats), jnp.float32),
            pltpu.SMEM((peers,), jnp.int32),
            pltpu.SemaphoreType.DMA((peers,)),
            pltpu.SemaphoreType.DMA((len(lanes),)),
        ],
        compiler_params=pltpu.CompilerParams(vmem_limit_bytes=32 * 1024 * 1024),
        cost_estimate=pl.CostEstimate(flops=6 * features.size, bytes_accessed=8 * features.size, transcendentals=0),
        name="pick_rest",
    )(dest, slot, pin(features))
    return res[0], res[1:]


def place_kernel(lanes, near_by, slot_ref, scale_ref, *rest):
    blocks, (out_ref, held, in_sems, out_sems) = rest[: len(lanes)], rest[-4:]
    _, parts, part_rows, _ = held.shape
    plan = []
    for n, lane in enumerate(lanes):
        start = jnp.max(slot_ref[lane : lane + 1, :]) * (parts * part_rows)
        for i in range(parts):
            target = pl.ds(pl.multiple_of(start + i * part_rows, 8), part_rows)
            source = blocks[n].at[pl.ds(i * part_rows, part_rows)]
            fetch = None if near_by else pltpu.make_async_copy(source, held.at[n, i], in_sems.at[n, i])
            if fetch is not None:
                fetch.start()
            plan.append((n, i, source, fetch, pltpu.make_async_copy(held.at[n, i], out_ref.at[target], out_sems.at[n, i])))
    center, factor = scale_ref[0:1], scale_ref[1:2]
    for n, i, source, fetch, store in plan:
        if fetch is not None:
            fetch.wait()
        values = source[...] if fetch is None else held[n, i]
        held[n, i] = jnp.clip((values - center) * factor, -clip_value, clip_value)
        store.start()
    for *_, store in plan:
        store.wait()


def place(lanes, blocks, slots, scale, out, row_count, near_by):
    rows, feats = blocks[0].shape
    count, parts = len(lanes), max(1, rows // 64)
    space, spec = (pltpu.VMEM, in_vmem) if near_by else (pltpu.HBM, in_hbm)
    args = [pin(slots, pltpu.VMEM), pin(scale, pltpu.VMEM)] + [pin(block, space) for block in blocks] + ([] if out is None else [pin(out)])
    return pl.pallas_call(
        functools.partial(place_kernel, lanes, near_by),
        out_shape=pltpu.HBM((row_count, feats), jnp.float32),
        in_specs=[in_vmem, in_vmem] + [spec] * count + ([] if out is None else [in_hbm]),
        out_specs=in_hbm,
        scratch_shapes=[
            pltpu.VMEM((count, parts, rows // parts, feats), jnp.float32),
            pltpu.SemaphoreType.DMA((count, parts)),
            pltpu.SemaphoreType.DMA((count, parts)),
        ],
        input_output_aliases={} if out is None else {2 + count: 0},
        compiler_params=pltpu.CompilerParams(vmem_limit_bytes=32 * 1024 * 1024),
        cost_estimate=pl.CostEstimate(flops=4 * count * rows * feats, bytes_accessed=8 * count * rows * feats, transcendentals=0),
        name="place",
    )(*args)


def merge_chunk(told, row_count, feats):
    peers, outer_count = told.shape[0], lax.axis_size("outer")
    chunk = feats // peers
    slots = told[:, 0, message_width - 128 :].astype(jnp.int32)[lane_base(peers) ^ jnp.arange(peers, dtype=jnp.int32)]
    level_count = row_count
    centers, spreads = told[:, 0, :chunk], told[:, 0, chunk : 2 * chunk]
    while centers.shape[0] > 1:
        centers, spreads = merge_pair(centers[0::2], spreads[0::2], centers[1::2], spreads[1::2], level_count * 0.5)
        level_count *= 2
    pair = jnp.concatenate([centers, spreads], axis=0)
    for bit in range(outer_count.bit_length() - 1):
        other = lax.ppermute(pair, "outer", [(i, i ^ 1 << bit) for i in range(outer_count)])
        center, spread = merge_pair(pair[0], pair[1], other[0], other[1], level_count * 0.5)
        level_count *= 2
        pair = jnp.stack([center, spread])
    return slots, jnp.broadcast_to(pair.reshape(1, 1, 2 * chunk), (peers, 1, 2 * chunk))


def spread_moments(shares, total_rows):
    chunk = shares.shape[2] // 2
    center, variance = shares[:, 0, :chunk].reshape(-1), shares[:, 0, chunk:].reshape(-1) / total_rows
    return center, variance, jnp.stack([center, lax.rsqrt(variance + eps_value)])


def body(features, dest, slot):
    row_count, feats = features.shape
    peers, outer_count = dest.shape[0], lax.axis_size("outer")
    order = lane_order(peers)
    first = pick_first(order[:head_count], dest, features)
    dest, slot, *first = lax.optimization_barrier((dest, slot, *first))
    payload, later = pick_rest(order[head_count:], order[:head_count], dest, slot, features)
    picked, got = list(first) + list(later), []

    def send(block, lane):
        pairs = [(o * peers + i, o * peers + (i ^ lane ^ (o & 1) * (peers // 2))) for o in range(outer_count) for i in range(peers)]
        return lax.ppermute(block, ("outer", "inner"), pairs)

    def place_lanes(begin, end, out, near_by=False):
        return place(order[begin:end], got[begin:end], slots, scale, out, row_count, near_by)

    out, placed = None, 0
    for j in range(peers):
        if j >= window:
            k = j - window
            extra = []
            if k == tell_step:
                extra = [payload]
            elif k == told_step:
                extra = [told]
            elif k == share_step:
                extra = [share]
            elif k == shared_step:
                extra = [shared]
            elif k in place_steps:
                out = place_lanes(placed, k, out)
                placed = k
                extra = [out]
            picked[j], got[k], *extra = lax.optimization_barrier((picked[j], got[k], *extra))
            if k == tell_step:
                told = lax.all_to_all(extra[0], "inner", split_axis=0, concat_axis=0, tiled=True)
            elif k == told_step:
                slots, share = merge_chunk(extra[0], row_count, feats)
            elif k == share_step:
                shared = lax.all_to_all(extra[0], "inner", split_axis=0, concat_axis=0, tiled=True)
            elif k == shared_step:
                center, variance, scale = spread_moments(extra[0], row_count * peers * outer_count)
            elif extra:
                out = extra[0]
        got.append(send(picked[j], order[j]))
    for begin, end in zip((placed,) + last_cuts(peers), last_cuts(peers) + (peers,)):
        out = place_lanes(begin, end, out, begin >= peers - 4)
    return (out, jnp.stack([center, variance]))


def solution(mesh):
    in_specs = (P(("outer", "inner"), None), P(("outer", "inner")), P(("outer", "inner")))
    out_specs = (P(("outer", "inner"), None), P())
    return jax.shard_map(body, mesh=mesh, in_specs=in_specs, out_specs=out_specs, check_vma=False)
```

```python
import functools

import jax
import jax.numpy as jnp
from jax import lax
from jax.experimental import pallas as pl
from jax.experimental.pallas import tpu as pltpu
from jax.sharding import PartitionSpec as P

eps_value = 1e-06
clip_value = 3.0
message_width = 256
window = 4
head_count = 2
tell_step = 1
told_step = 5
share_step = 7
shared_step = 9
place_steps = (10,)
in_smem, in_vmem = pl.BlockSpec(memory_space=pltpu.SMEM), pl.BlockSpec(memory_space=pltpu.VMEM)
in_hbm, in_any = pl.BlockSpec(memory_space=pltpu.HBM), pl.BlockSpec(memory_space=pl.ANY)


def merge_pair(center_a, spread_a, center_b, spread_b, half):
    gap = center_b - center_a
    return ((center_a + center_b) * 0.5, spread_a + spread_b + gap * gap * half)


def pin(array, space=pltpu.HBM):
    return pltpu.with_memory_space_constraint(array, space)


def lane_order(peers):
    half, quarter = peers // 2, peers // 4
    far = [half + k for k in (*range(0, half, 2), *range(1, half, 2))]
    far[-2:] = far[:-3:-1]
    near = [*range(1, half, 2), *range(2, half, 2), 0]
    at = near.index(quarter)
    near[0], near[at] = quarter, near[0]
    return [lane for pair in zip(far, near) for lane in pair]


def last_cuts(peers):
    return (peers - 4, peers - 2)


def lane_base(peers):
    return lax.axis_index("inner") ^ ((lax.axis_index("outer") & 1) * (peers // 2))


def invert(dest_ref, inverse):
    peers = dest_ref.shape[0]
    base = lane_base(peers)
    for b in range(peers):
        inverse[dest_ref[b] ^ base] = b
    return base


def first_kernel(lanes, dest_ref, features_ref, *rest):
    outs, (inverse, sems) = rest[:-2], rest[-2:]
    rows, parts = outs[0].shape[0], sems.shape[1]
    invert(dest_ref, inverse)
    copies = []
    for i, lane in enumerate(lanes):
        for p in range(parts):
            start = pl.multiple_of(inverse[lane] * rows + p * (rows // parts), 8)
            target = outs[i].at[pl.ds(p * (rows // parts), rows // parts)]
            copies.append(pltpu.make_async_copy(features_ref.at[pl.ds(start, rows // parts)], target, sems.at[i, p]))
            copies[-1].start()
    for copy in copies:
        copy.wait()


def pick_first(lanes, dest, features):
    count, (row_count, feats) = len(lanes), features.shape
    rows = row_count // dest.shape[0]
    return pl.pallas_call(
        functools.partial(first_kernel, lanes),
        out_shape=[pltpu.VMEM((rows, feats), features.dtype)] * count,
        in_specs=[in_smem, in_hbm],
        out_specs=[in_vmem] * count,
        scratch_shapes=[pltpu.SMEM(dest.shape, jnp.int32), pltpu.SemaphoreType.DMA((count, 1))],
        name="pick_first",
    )(dest, pin(features))


def rest_kernel(lanes, first, dest_ref, slot_ref, features_ref, payload_ref, *rest):
    outs, (held, inverse_ref, in_sems, out_sems) = rest[: len(lanes)], rest[len(lanes) :]
    peers, rows, feats = held.shape
    base = invert(dest_ref, inverse_ref)
    order = lanes + first
    fetches = []
    for lane in order:
        start = pl.multiple_of(inverse_ref[lane] * rows, 8)
        fetches.append(pltpu.make_async_copy(features_ref.at[pl.ds(start, rows)], held.at[lane], in_sems.at[lane]))
        fetches[-1].start()

    def fold(x):
        return jnp.sum(x.reshape(rows // 8, 8, feats), axis=0)

    stores, parts = [], []
    for i, lane in enumerate(order):
        fetches[i].wait()
        if i < len(lanes):
            stores.append(pltpu.make_async_copy(held.at[lane], outs[i], out_sems.at[i]))
            stores[-1].start()
        center = jnp.sum(fold(held[lane]), axis=0, keepdims=True) / rows
        gap = held[lane] - center
        parts.append((center, jnp.sum(fold(gap * gap), axis=0, keepdims=True)))
    level_count = rows
    while len(parts) > 1:
        parts = [merge_pair(*parts[i], *parts[i + 1], level_count * 0.5) for i in range(0, len(parts), 2)]
        level_count *= 2
    center, spread = parts[0]
    chunk = feats // peers
    for peer in range(peers):
        mark = jnp.full((1, payload_ref.shape[2] - 2 * chunk), slot_ref[inverse_ref[peer ^ base]].astype(jnp.float32))
        pieces = [x[:, peer * chunk : (peer + 1) * chunk] for x in (center, spread)]
        payload_ref[peer] = jnp.concatenate(pieces + [mark], axis=1)
    for store in stores:
        store.wait()


def pick_rest(lanes, first, dest, slot, features):
    peers, (row_count, feats) = dest.shape[0], features.shape
    rows = row_count // peers
    res = pl.pallas_call(
        functools.partial(rest_kernel, lanes, first),
        out_shape=[jax.ShapeDtypeStruct((peers, 1, message_width), jnp.float32)] + [pltpu.HBM((rows, feats), features.dtype)] * len(lanes),
        in_specs=[in_smem, in_smem, in_hbm],
        out_specs=[in_vmem] + [in_hbm] * len(lanes),
        scratch_shapes=[
            pltpu.VMEM((peers, rows, feats), jnp.float32),
            pltpu.SMEM((peers,), jnp.int32),
            pltpu.SemaphoreType.DMA((peers,)),
            pltpu.SemaphoreType.DMA((len(lanes),)),
        ],
        compiler_params=pltpu.CompilerParams(vmem_limit_bytes=32 * 1024 * 1024),
        name="pick_rest",
    )(dest, slot, pin(features))
    return res[0], res[1:]


def place_kernel(lanes, near_by, slot_ref, scale_ref, *rest):
    blocks, (out_ref, held, in_sems, out_sems) = rest[: len(lanes)], rest[-4:]
    _, parts, part_rows, _ = held.shape
    plan = []
    for n, lane in enumerate(lanes):
        start = jnp.max(slot_ref[lane : lane + 1, :]) * (parts * part_rows)
        for i in range(parts):
            target = pl.ds(pl.multiple_of(start + i * part_rows, 8), part_rows)
            source = blocks[n].at[pl.ds(i * part_rows, part_rows)]
            fetch = None if near_by else pltpu.make_async_copy(source, held.at[n, i], in_sems.at[n, i])
            if fetch is not None:
                fetch.start()
            plan.append((n, i, source, fetch, pltpu.make_async_copy(held.at[n, i], out_ref.at[target], out_sems.at[n, i])))
    center, factor = scale_ref[0:1], scale_ref[1:2]
    for n, i, source, fetch, store in plan:
        if fetch is not None:
            fetch.wait()
        values = source[...] if fetch is None else held[n, i]
        held[n, i] = jnp.clip((values - center) * factor, -clip_value, clip_value)
        store.start()
    for *_, store in plan:
        store.wait()


def place(lanes, blocks, slots, scale, out, row_count, near_by):
    rows, feats = blocks[0].shape
    count, parts = len(lanes), max(1, rows // 64)
    space, spec = (pltpu.VMEM, in_vmem) if near_by else (pltpu.HBM, in_hbm)
    args = [pin(slots, pltpu.VMEM), pin(scale, pltpu.VMEM)] + [pin(block, space) for block in blocks] + ([] if out is None else [pin(out)])
    return pl.pallas_call(
        functools.partial(place_kernel, lanes, near_by),
        out_shape=pltpu.HBM((row_count, feats), jnp.float32),
        in_specs=[in_vmem, in_vmem] + [spec] * count + ([] if out is None else [in_hbm]),
        out_specs=in_hbm,
        scratch_shapes=[
            pltpu.VMEM((count, parts, rows // parts, feats), jnp.float32),
            pltpu.SemaphoreType.DMA((count, parts)),
            pltpu.SemaphoreType.DMA((count, parts)),
        ],
        input_output_aliases={} if out is None else {2 + count: 0},
        compiler_params=pltpu.CompilerParams(vmem_limit_bytes=32 * 1024 * 1024),
        cost_estimate=pl.CostEstimate(flops=4 * count * rows * feats, bytes_accessed=8 * count * rows * feats, transcendentals=0),
        name="place",
    )(*args)


def merge_chunk(told, row_count, feats):
    peers, outer_count = told.shape[0], lax.axis_size("outer")
    chunk = feats // peers
    slots = told[:, 0, message_width - 128 :].astype(jnp.int32)[lane_base(peers) ^ jnp.arange(peers, dtype=jnp.int32)]
    level_count = row_count
    centers, spreads = told[:, 0, :chunk], told[:, 0, chunk : 2 * chunk]
    while centers.shape[0] > 1:
        centers, spreads = merge_pair(centers[0::2], spreads[0::2], centers[1::2], spreads[1::2], level_count * 0.5)
        level_count *= 2
    pair = jnp.concatenate([centers, spreads], axis=0)
    for bit in range(outer_count.bit_length() - 1):
        other = lax.ppermute(pair, "outer", [(i, i ^ 1 << bit) for i in range(outer_count)])
        center, spread = merge_pair(pair[0], pair[1], other[0], other[1], level_count * 0.5)
        level_count *= 2
        pair = jnp.stack([center, spread])
    return slots, jnp.broadcast_to(pair.reshape(1, 1, 2 * chunk), (peers, 1, 2 * chunk))


def spread_moments(shares, total_rows):
    chunk = shares.shape[2] // 2
    center, variance = shares[:, 0, :chunk].reshape(-1), shares[:, 0, chunk:].reshape(-1) / total_rows
    return center, variance, jnp.stack([center, lax.rsqrt(variance + eps_value)])


def body(features, dest, slot):
    row_count, feats = features.shape
    peers, outer_count = dest.shape[0], lax.axis_size("outer")
    order = lane_order(peers)
    first = pick_first(order[:head_count], dest, features)
    dest, slot, *first = lax.optimization_barrier((dest, slot, *first))
    payload, later = pick_rest(order[head_count:], order[:head_count], dest, slot, features)
    picked, got = list(first) + list(later), []

    def send(block, lane):
        pairs = [(o * peers + i, o * peers + (i ^ lane ^ (o & 1) * (peers // 2))) for o in range(outer_count) for i in range(peers)]
        return lax.ppermute(block, ("outer", "inner"), pairs)

    def place_lanes(begin, end, out, near_by=False):
        return place(order[begin:end], got[begin:end], slots, scale, out, row_count, near_by)

    out, placed = None, 0
    for j in range(peers):
        if j >= window:
            k = j - window
            extra = []
            if k == tell_step:
                extra = [payload]
            elif k == told_step:
                extra = [told]
            elif k == share_step:
                extra = [share]
            elif k == shared_step:
                extra = [shared]
            elif k in place_steps:
                out = place_lanes(placed, k, out)
                placed = k
                extra = [out]
            picked[j], got[k], *extra = lax.optimization_barrier((picked[j], got[k], *extra))
            if k == tell_step:
                told = lax.all_to_all(extra[0], "inner", split_axis=0, concat_axis=0, tiled=True)
            elif k == told_step:
                slots, share = merge_chunk(extra[0], row_count, feats)
            elif k == share_step:
                shared = lax.all_to_all(extra[0], "inner", split_axis=0, concat_axis=0, tiled=True)
            elif k == shared_step:
                center, variance, scale = spread_moments(extra[0], row_count * peers * outer_count)
            elif extra:
                out = extra[0]
        got.append(send(picked[j], order[j]))
    for begin, end in zip((placed,) + last_cuts(peers), last_cuts(peers) + (peers,)):
        out = place_lanes(begin, end, out, begin >= peers - 4)
    return (out, jnp.stack([center, variance]))


def solution(mesh):
    in_specs = (P(("outer", "inner"), None), P(("outer", "inner")), P(("outer", "inner")))
    out_specs = (P(("outer", "inner"), None), P())
    return jax.shard_map(body, mesh=mesh, in_specs=in_specs, out_specs=out_specs, check_vma=False)
```

```python
import functools

import jax
import jax.numpy as jnp
from jax import lax
from jax.experimental import pallas as pl
from jax.experimental.pallas import tpu as pltpu
from jax.sharding import PartitionSpec as P

eps_value = 1e-06
clip_value = 3.0
message_width = 256
window = 4
head_count = 2
tell_step = 1
told_step = 5
share_step = 7
shared_step = 9
place_steps = (10,)
in_smem, in_vmem = pl.BlockSpec(memory_space=pltpu.SMEM), pl.BlockSpec(memory_space=pltpu.VMEM)
in_hbm, in_any = pl.BlockSpec(memory_space=pltpu.HBM), pl.BlockSpec(memory_space=pl.ANY)


def merge_pair(center_a, spread_a, center_b, spread_b, half):
    gap = center_b - center_a
    return ((center_a + center_b) * 0.5, spread_a + spread_b + gap * gap * half)


def pin(array, space=pltpu.HBM):
    return pltpu.with_memory_space_constraint(array, space)


def lane_order(peers):
    half, quarter = peers // 2, peers // 4
    far = [half + k for k in (*range(0, half, 2), *range(1, half, 2))]
    far[-2:] = far[:-3:-1]
    far[1], far[3] = far[3], far[1]
    near = [*range(1, half, 2), *range(2, half, 2), 0]
    at = near.index(quarter)
    near[0], near[at] = quarter, near[0]
    return [lane for pair in zip(far, near) for lane in pair]


def last_cuts(peers):
    return (peers - 4, peers - 2)


def lane_base(peers):
    return lax.axis_index("inner") ^ ((lax.axis_index("outer") & 1) * (peers // 2))


def invert(dest_ref, inverse):
    peers = dest_ref.shape[0]
    base = lane_base(peers)
    for b in range(peers):
        inverse[dest_ref[b] ^ base] = b
    return base


def first_kernel(lanes, dest_ref, features_ref, *rest):
    outs, (inverse, sems) = rest[:-2], rest[-2:]
    rows, parts = outs[0].shape[0], sems.shape[1]
    invert(dest_ref, inverse)
    copies = []
    for i, lane in enumerate(lanes):
        for p in range(parts):
            start = pl.multiple_of(inverse[lane] * rows + p * (rows // parts), 8)
            target = outs[i].at[pl.ds(p * (rows // parts), rows // parts)]
            copies.append(pltpu.make_async_copy(features_ref.at[pl.ds(start, rows // parts)], target, sems.at[i, p]))
            copies[-1].start()
    for copy in copies:
        copy.wait()


def pick_first(lanes, dest, features):
    count, (row_count, feats) = len(lanes), features.shape
    rows = row_count // dest.shape[0]
    return pl.pallas_call(
        functools.partial(first_kernel, lanes),
        out_shape=[pltpu.VMEM((rows, feats), features.dtype)] * count,
        in_specs=[in_smem, in_hbm],
        out_specs=[in_vmem] * count,
        scratch_shapes=[pltpu.SMEM(dest.shape, jnp.int32), pltpu.SemaphoreType.DMA((count, 1))],
        name="pick_first",
    )(dest, pin(features))


def rest_kernel(lanes, first, dest_ref, slot_ref, features_ref, payload_ref, *rest):
    outs, (held, inverse_ref, in_sems, out_sems) = rest[: len(lanes)], rest[len(lanes) :]
    peers, rows, feats = held.shape
    base = invert(dest_ref, inverse_ref)
    order = lanes + first
    fetches = []
    for lane in order:
        start = pl.multiple_of(inverse_ref[lane] * rows, 8)
        fetches.append(pltpu.make_async_copy(features_ref.at[pl.ds(start, rows)], held.at[lane], in_sems.at[lane]))
        fetches[-1].start()

    def fold(x):
        return jnp.sum(x.reshape(rows // 8, 8, feats), axis=0)

    stores, parts = [], []
    for i, lane in enumerate(order):
        fetches[i].wait()
        if i < len(lanes):
            stores.append(pltpu.make_async_copy(held.at[lane], outs[i], out_sems.at[i]))
            stores[-1].start()
        center = jnp.sum(fold(held[lane]), axis=0, keepdims=True) / rows
        gap = held[lane] - center
        parts.append((center, jnp.sum(fold(gap * gap), axis=0, keepdims=True)))
    level_count = rows
    while len(parts) > 1:
        parts = [merge_pair(*parts[i], *parts[i + 1], level_count * 0.5) for i in range(0, len(parts), 2)]
        level_count *= 2
    center, spread = parts[0]
    chunk = feats // peers
    for peer in range(peers):
        mark = jnp.full((1, payload_ref.shape[2] - 2 * chunk), slot_ref[inverse_ref[peer ^ base]].astype(jnp.float32))
        pieces = [x[:, peer * chunk : (peer + 1) * chunk] for x in (center, spread)]
        payload_ref[peer] = jnp.concatenate(pieces + [mark], axis=1)
    for store in stores:
        store.wait()


def pick_rest(lanes, first, dest, slot, features):
    peers, (row_count, feats) = dest.shape[0], features.shape
    rows = row_count // peers
    res = pl.pallas_call(
        functools.partial(rest_kernel, lanes, first),
        out_shape=[jax.ShapeDtypeStruct((peers, 1, message_width), jnp.float32)] + [pltpu.HBM((rows, feats), features.dtype)] * len(lanes),
        in_specs=[in_smem, in_smem, in_hbm],
        out_specs=[in_vmem] + [in_hbm] * len(lanes),
        scratch_shapes=[
            pltpu.VMEM((peers, rows, feats), jnp.float32),
            pltpu.SMEM((peers,), jnp.int32),
            pltpu.SemaphoreType.DMA((peers,)),
            pltpu.SemaphoreType.DMA((len(lanes),)),
        ],
        compiler_params=pltpu.CompilerParams(vmem_limit_bytes=32 * 1024 * 1024),
        cost_estimate=pl.CostEstimate(flops=6 * features.size, bytes_accessed=8 * features.size, transcendentals=0),
        name="pick_rest",
    )(dest, slot, pin(features))
    return res[0], res[1:]


def place_kernel(lanes, near_by, slot_ref, scale_ref, *rest):
    blocks, (out_ref, held, in_sems, out_sems) = rest[: len(lanes)], rest[-4:]
    _, parts, part_rows, _ = held.shape
    plan = []
    for n, lane in enumerate(lanes):
        start = jnp.max(slot_ref[lane : lane + 1, :]) * (parts * part_rows)
        for i in range(parts):
            target = pl.ds(pl.multiple_of(start + i * part_rows, 8), part_rows)
            source = blocks[n].at[pl.ds(i * part_rows, part_rows)]
            fetch = None if near_by else pltpu.make_async_copy(source, held.at[n, i], in_sems.at[n, i])
            if fetch is not None:
                fetch.start()
            plan.append((n, i, source, fetch, pltpu.make_async_copy(held.at[n, i], out_ref.at[target], out_sems.at[n, i])))
    center, factor = scale_ref[0:1], scale_ref[1:2]
    for n, i, source, fetch, store in plan:
        if fetch is not None:
            fetch.wait()
        values = source[...] if fetch is None else held[n, i]
        held[n, i] = jnp.clip((values - center) * factor, -clip_value, clip_value)
        store.start()
    for *_, store in plan:
        store.wait()


def place(lanes, blocks, slots, scale, out, row_count, near_by):
    rows, feats = blocks[0].shape
    count, parts = len(lanes), max(1, rows // 64)
    space, spec = (pltpu.VMEM, in_vmem) if near_by else (pltpu.HBM, in_hbm)
    args = [pin(slots, pltpu.VMEM), pin(scale, pltpu.VMEM)] + [pin(block, space) for block in blocks] + ([] if out is None else [pin(out)])
    return pl.pallas_call(
        functools.partial(place_kernel, lanes, near_by),
        out_shape=pltpu.HBM((row_count, feats), jnp.float32),
        in_specs=[in_vmem, in_vmem] + [spec] * count + ([] if out is None else [in_hbm]),
        out_specs=in_hbm,
        scratch_shapes=[
            pltpu.VMEM((count, parts, rows // parts, feats), jnp.float32),
            pltpu.SemaphoreType.DMA((count, parts)),
            pltpu.SemaphoreType.DMA((count, parts)),
        ],
        input_output_aliases={} if out is None else {2 + count: 0},
        compiler_params=pltpu.CompilerParams(vmem_limit_bytes=32 * 1024 * 1024),
        cost_estimate=pl.CostEstimate(flops=4 * count * rows * feats, bytes_accessed=8 * count * rows * feats, transcendentals=0),
        name="place",
    )(*args)


def merge_chunk(told, row_count, feats):
    peers, outer_count = told.shape[0], lax.axis_size("outer")
    chunk = feats // peers
    slots = told[:, 0, message_width - 128 :].astype(jnp.int32)[lane_base(peers) ^ jnp.arange(peers, dtype=jnp.int32)]
    level_count = row_count
    centers, spreads = told[:, 0, :chunk], told[:, 0, chunk : 2 * chunk]
    while centers.shape[0] > 1:
        centers, spreads = merge_pair(centers[0::2], spreads[0::2], centers[1::2], spreads[1::2], level_count * 0.5)
        level_count *= 2
    pair = jnp.concatenate([centers, spreads], axis=0)
    for bit in range(outer_count.bit_length() - 1):
        other = lax.ppermute(pair, "outer", [(i, i ^ 1 << bit) for i in range(outer_count)])
        center, spread = merge_pair(pair[0], pair[1], other[0], other[1], level_count * 0.5)
        level_count *= 2
        pair = jnp.stack([center, spread])
    return slots, jnp.broadcast_to(pair.reshape(1, 1, 2 * chunk), (peers, 1, 2 * chunk))


def spread_moments(shares, total_rows):
    chunk = shares.shape[2] // 2
    center, variance = shares[:, 0, :chunk].reshape(-1), shares[:, 0, chunk:].reshape(-1) / total_rows
    return center, variance, jnp.stack([center, lax.rsqrt(variance + eps_value)])


def body(features, dest, slot):
    row_count, feats = features.shape
    peers, outer_count = dest.shape[0], lax.axis_size("outer")
    order = lane_order(peers)
    first = pick_first(order[:head_count], dest, features)
    dest, slot, *first = lax.optimization_barrier((dest, slot, *first))
    payload, later = pick_rest(order[head_count:], order[:head_count], dest, slot, features)
    picked, got = list(first) + list(later), []

    def send(block, lane):
        pairs = [(o * peers + i, o * peers + (i ^ lane ^ (o & 1) * (peers // 2))) for o in range(outer_count) for i in range(peers)]
        return lax.ppermute(block, ("outer", "inner"), pairs)

    def place_lanes(begin, end, out, near_by=False):
        return place(order[begin:end], got[begin:end], slots, scale, out, row_count, near_by)

    out, placed = None, 0
    for j in range(peers):
        if j >= window:
            k = j - window
            extra = []
            if k == tell_step:
                extra = [payload]
            elif k == told_step:
                extra = [told]
            elif k == share_step:
                extra = [share]
            elif k == shared_step:
                extra = [shared]
            elif k in place_steps:
                out = place_lanes(placed, k, out)
                placed = k
                extra = [out]
            picked[j], got[k], *extra = lax.optimization_barrier((picked[j], got[k], *extra))
            if k == tell_step:
                told = lax.all_to_all(extra[0], "inner", split_axis=0, concat_axis=0, tiled=True)
            elif k == told_step:
                slots, share = merge_chunk(extra[0], row_count, feats)
            elif k == share_step:
                shared = lax.all_to_all(extra[0], "inner", split_axis=0, concat_axis=0, tiled=True)
            elif k == shared_step:
                center, variance, scale = spread_moments(extra[0], row_count * peers * outer_count)
            elif extra:
                out = extra[0]
        got.append(send(picked[j], order[j]))
    for begin, end in zip((placed,) + last_cuts(peers), last_cuts(peers) + (peers,)):
        out = place_lanes(begin, end, out, begin >= peers - 4)
    return (out, jnp.stack([center, variance]))


def solution(mesh):
    in_specs = (P(("outer", "inner"), None), P(("outer", "inner")), P(("outer", "inner")))
    out_specs = (P(("outer", "inner"), None), P())
    return jax.shard_map(body, mesh=mesh, in_specs=in_specs, out_specs=out_specs, check_vma=False)
```
